256 devices in a mesh: seq: 32 (over x, z), head: 8 (over y, core).
Axes of the slice: x: 4, y: 4, z: 8, core: 2. Of those that a mesh axis runs over, the one named last changes fastest.
Arguments:
- queries: bfloat16 [16384, 4096], P('seq', 'head'), may hold values from -8 to 8
- key_rows: bfloat16 [16384, 512], P('seq'), may hold values from -8 to 8
- value_rows: bfloat16 [16384, 512], P('seq'), may hold values from -6 to 6
- doc_lengths: int32 [128], replicated, may hold values from 1 to 256, 16384 in all
- residual_in: bfloat16 [16384, 2048], P(('seq', 'head')), may hold values from -6 to 6
- out_weight: bfloat16 [4096, 2048], P('head'), may hold values from -0.09375 to 0.09375
- norm_gain: float32 [2048], replicated, may hold values from 0.5 to 1.5
- expert_ids: int32 [16384, 8], P(('seq', 'head')), may hold values from 0 to 127, all different within a row; in each aligned block of 64 rows (0 to 63, 64 to 127, ...) at most 5 rows name the same one
- gate_weights: float32 [16384, 8], P(('seq', 'head')), may hold values from 0.05 to 0.3
- w_gate: bfloat16 [256, 2048, 384], P(('seq', 'head')), may hold values from -0.125 to 0.125
- w_up: bfloat16 [256, 2048, 384], P(('seq', 'head')), may hold values from -0.125 to 0.125
- w_down: bfloat16 [256, 384, 2048], P(('seq', 'head')), may hold values from -0.21875 to 0.21875
Outputs:
- layer_out: bfloat16 [16384, 2048], P(('seq', 'head'))
The draws below stay inside these ranges and needn't reach their ends.
Inputs may be any that keep to these rules, and one draw needn't show every extreme that they name: `doc_lengths`: the lengths sum to 16384 and the longest is exactly 256. `expert_ids`: a token names 8 different experts; among the 64 tokens of one device, in aligned blocks in order, no expert is named by more than 5 of them, a bound that some block reaches.
All inputs are finite; a program needn't handle non-finite values.
Results may differ from the reference program's by a relative error of at most 0.011.
Values may be sent and summed in bfloat16 or wider, within the bound.
No kernel may reach another device: no remote copies, remote signals or barrier semaphores. Data moves between devices by JAX's collectives and lax.ppermute only.
A program may use at most 128 MiB of HBM per device.

```python
import math
import jax
import jax.numpy as jnp
import numpy as np
from jax import lax

D = 2048
FF = 768
HQ = 32
KVH = 4
HD = 128
TOPK = 8
TOK_DEV = 512
TOKENS = 16384
NDOCS = 128
MAXDOC = 256
ROWS_DEV = 64
EXPERTS = 128
CAP = 5
N_SEQ = 32


def draw_queries(key, part):
    key = jax.random.fold_in(key, 7)
    drawn = jnp.clip(jax.random.normal(key, (TOKENS, HQ * HD), jnp.float32), -8.0, 8.0)
    return drawn.astype(jnp.bfloat16)


def draw_key_rows(key, part):
    key = jax.random.fold_in(key, 9)
    drawn = jnp.clip(jax.random.normal(key, (TOKENS, KVH * HD), jnp.float32), -8.0, 8.0)
    return drawn.astype(jnp.bfloat16)


def level_of(stream_key, shape, pieces, low, top_value):
    def one(dim, shards_of):
        steps = jax.random.uniform(jax.random.fold_in(jax.random.fold_in(stream_key, 6), dim), (shards_of,), jnp.float32, low / len(pieces), top_value / len(pieces))
        return jnp.repeat(jnp.exp(steps), shape[dim] // shards_of).reshape((-1,) + (1,) * (len(shape) - dim - 1))

    factor_of = one(*pieces[0])
    for cut in pieces[1:]:
        factor_of = factor_of * one(*cut)
    return factor_of


def length_profile(amount, total, limit, slope):
    weights = [(1 << 20) // math.isqrt(grade ** slope) + 1 for grade in range(2, amount + 1)]
    rest, counts = total - limit - (amount - 1), [1] * (amount - 1)
    while rest > 0:
        movable = [i for i in range(amount - 1) if counts[i] < limit]
        mass, budget = sum([weights[i] for i in movable]), rest
        for i in movable:
            more = min(limit - counts[i], max(1, budget * weights[i] // mass), rest)
            counts[i] = counts[i] + more
            rest = rest - more
    return np.array([limit] + counts)


def ragged_sizes(rng, amount, total, limit, skew):
    if amount == 2:
        one = jax.random.randint(rng, (), max(1, total - limit), min(limit, total - 1) + 1)
        return jnp.stack([one, total - one])
    tallies = jnp.asarray(length_profile(amount, total, limit, skew), jnp.int32)
    twos = (amount - 1) // 2
    donor, taker = tallies[1:1 + 2 * twos:2], tallies[2:2 + 2 * twos:2]
    room = jnp.minimum(donor - 1, limit - taker)
    shifted = jax.random.randint(jax.random.fold_in(rng, 1), (twos,), 0, 1 << 20) % (room + 1)
    tallies = tallies.at[1:1 + 2 * twos:2].set(donor - shifted).at[2:2 + 2 * twos:2].set(taker + shifted)
    return tallies[jax.random.permutation(jax.random.fold_in(rng, 2), amount)]


def assign_block(key, own, number, rows, amount, top, bound, skew):
    sequence = jax.random.permutation(key, amount)
    heavy_load, ordinary = load_shares(amount, rows * top, bound, skew, True), load_shares(amount, rows * top, bound, skew, False)
    places = jnp.arange(amount)

    def named(lengths, offset_by):
        used = int((lengths > 0).sum())
        fixed = max(1, used // 4)
        passed = fixed + (places - fixed + offset_by * (used - fixed)) % max(1, amount - fixed)
        return jnp.zeros((amount,), jnp.int32).at[sequence[jnp.where(places < fixed, places, passed)]].set(jnp.asarray(lengths, jnp.int32))

    lengths = jnp.where(number % 4 == 0, named(heavy_load, number // 4), named(ordinary, number - number // 4 - 1))
    mixed = jax.random.permutation(jax.random.fold_in(own, 3), amount)
    source_of, taker = mixed[0:amount // 2 * 2:2], mixed[1:amount // 2 * 2:2]
    room = jnp.minimum(lengths[source_of] - 1, bound - lengths[taker]) // 2
    room = jnp.where((source_of == sequence[0]) | (taker == sequence[0]) | (lengths[taker] == 0), 0, jnp.maximum(room, 0))
    passed = jax.random.randint(jax.random.fold_in(own, 4), (amount // 2,), 0, 1 << 20) % (room + 1)
    lengths = lengths.at[source_of].add(-passed).at[taker].add(passed)
    labels = jnp.searchsorted(jnp.cumsum(lengths), jnp.arange(rows * top), side="right").astype(jnp.int32)
    listing = labels.reshape(top, rows).T
    listing = listing[jax.random.permutation(jax.random.fold_in(own, 1), rows)]
    offset_by = jax.random.randint(jax.random.fold_in(own, 2), (rows, 1), 0, top)
    return jnp.take_along_axis(listing, (jnp.arange(top)[None, :] + offset_by) % top, axis=1)


def load_shares(number_of, total, limit, skew, full):
    weights = [(1 << 20) // math.isqrt(standing ** skew) + 1 for standing in range(1, number_of + 1)]
    largest = limit if full else min(limit, max(-(-total // number_of), total * weights[0] // sum(weights)))
    least = 1 if total - largest >= number_of - 1 else 0
    given, spare = [largest] + [least] * (number_of - 1), total - largest - least * (number_of - 1)
    while spare > 0:
        free = [i for i in range(1, number_of) if given[i] < largest] or [i for i in range(1, number_of) if given[i] < limit]
        mass, left = sum([weights[i] for i in free]), spare
        for i in free:
            more = min(limit - given[i], max(1, left * weights[i] // mass), spare)
            given[i] = given[i] + more
            spare = spare - more
    return np.array(given)


def scatter_about(own_key, extent, scale, limit, shards=(), held_as=jnp.bfloat16):
    result = scale * jax.random.normal(own_key, extent, jnp.float32)
    if shards:
        result = result * level_of(own_key, extent, shards, -0.22, 0.18)
    return jnp.clip(result, -limit, limit).astype(held_as)


def setup_inputs(seed: int = 0) -> dict:
    splits = jax.random.split(jax.random.key(seed), 13)
    queries = draw_queries(jax.random.fold_in(splits[12], 71), 0)
    key_rows = draw_key_rows(jax.random.fold_in(splits[12], 71), 0)
    value_rows = scatter_about(splits[2], (TOKENS, KVH * HD), 1.0, 6.0, ((0, 32),))
    doc_lengths = ragged_sizes(splits[3], NDOCS, TOKENS, MAXDOC, 2).astype(jnp.int32)
    residual_in = scatter_about(splits[4], (TOKENS, D), 1.0, 6.0, ((0, 256),))
    out_weight = scatter_about(splits[5], (HQ * HD, D), (HQ * HD) ** -0.5, 0.09375, ((0, 8),))
    norm_gain = jnp.clip(1.0 + 0.1 * jax.random.normal(splits[6], (D,), jnp.float32), 0.5, 1.5)
    expert_ids_keys = jax.random.split(jax.random.fold_in(splits[7], 1), TOKENS // ROWS_DEV)
    expert_ids_turns = jax.random.permutation(jax.random.fold_in(splits[7], 3), TOKENS // ROWS_DEV)
    expert_ids = jax.vmap(lambda own, number: assign_block(jax.random.fold_in(splits[7], 2), own, number, ROWS_DEV, EXPERTS, TOPK, CAP, 2))(expert_ids_keys, expert_ids_turns).reshape((TOKENS, TOPK))
    gate_weights = jnp.clip(0.05 + 0.25 * jax.random.uniform(splits[8], (TOKENS, TOPK), jnp.float32) ** level_of(splits[8], (TOKENS, TOPK), ((0, 256),), -0.2, 0.2), 0.05, 0.3)
    w_gate = scatter_about(splits[9], (EXPERTS * 2, D, FF // 2), D ** -0.5, 0.125, ((0, 256),))
    w_up = scatter_about(splits[10], (EXPERTS * 2, D, FF // 2), D ** -0.5, 0.125, ((0, 256),))
    w_down = scatter_about(splits[11], (EXPERTS * 2, FF // 2, D), FF ** -0.5, 0.21875, ((0, 256),))
    return {"queries": queries, "key_rows": key_rows, "value_rows": value_rows, "doc_lengths": doc_lengths, "residual_in": residual_in, "out_weight": out_weight, "norm_gain": norm_gain, "expert_ids": expert_ids, "gate_weights": gate_weights, "w_gate": w_gate, "w_up": w_up, "w_down": w_down}


masked_low = -1e+30

def doc_index(positions, doc_lengths):
    doc_ends = jnp.cumsum(doc_lengths)
    return lax.optimization_barrier(jnp.sum((positions[:, None] >= doc_ends[None, :]).astype(jnp.int32), axis=1))

def reference(queries, key_rows, value_rows, doc_lengths, residual_in, out_weight, norm_gain, expert_ids, gate_weights, w_gate, w_up, w_down):
    group_size = HQ // KVH
    score_scale = 1.0 / math.sqrt(HD)
    window = MAXDOC + TOK_DEV
    padded_keys = jnp.concatenate([jnp.zeros((MAXDOC, KVH * HD), jnp.bfloat16), key_rows], axis=0)
    padded_values = jnp.concatenate([jnp.zeros((MAXDOC, KVH * HD), jnp.bfloat16), value_rows], axis=0)

    def attend_block(block_index):
        starting_position = (block_index * TOK_DEV).astype(jnp.int32)
        query_pos = starting_position + jnp.arange(TOK_DEV, dtype=jnp.int32)
        query_doc = doc_index(query_pos, doc_lengths)
        key_pos = starting_position - MAXDOC + jnp.arange(window, dtype=jnp.int32)
        key_doc = doc_index(key_pos, doc_lengths)
        query_heads = lax.dynamic_slice_in_dim(queries, starting_position, TOK_DEV, 0).reshape(TOK_DEV, HQ, HD).astype(jnp.float32)
        key_block = lax.dynamic_slice_in_dim(padded_keys, starting_position, window, 0).reshape(window, KVH, HD)
        value_block = lax.dynamic_slice_in_dim(padded_values, starting_position, window, 0).reshape(window, KVH, HD)
        key_heads = jnp.repeat(key_block, group_size, axis=1).astype(jnp.float32)
        value_head_rows = jnp.repeat(value_block, group_size, axis=1).astype(jnp.float32)
        scores = jnp.einsum('qhd,khd->hqk', query_heads, key_heads) * score_scale
        visible = (key_pos[None, :] <= query_pos[:, None]) & (key_doc[None, :] == query_doc[:, None]) & (key_pos[None, :] >= 0)
        visible = visible[None]
        row_top = lax.optimization_barrier(jnp.max(jnp.where(visible, scores, masked_low), axis=2, keepdims=True))
        weights = jnp.exp(jnp.where(visible, scores - row_top, masked_low))
        totals = lax.optimization_barrier(jnp.sum(weights, axis=2))
        rounded = weights.astype(jnp.bfloat16).astype(jnp.float32)
        mixture = jnp.einsum('hqk,khd->hqd', rounded, value_head_rows)
        attention_result = (mixture / totals[:, :, None]).astype(jnp.bfloat16)
        return attention_result.transpose(1, 0, 2).reshape(TOK_DEV, HQ * HD)
    attn = lax.map(attend_block, jnp.arange(N_SEQ, dtype=jnp.int32)).reshape(TOKENS, HQ * HD)
    projected = jnp.dot(attn, out_weight, preferred_element_type=jnp.float32)
    mid = residual_in.astype(jnp.float32) + projected
    spread = lax.optimization_barrier(jnp.mean(mid * mid, axis=1, keepdims=True))
    normed = (mid * lax.rsqrt(spread + 1e-06) * norm_gain[None, :]).astype(jnp.bfloat16)
    flat_ids = expert_ids.reshape(-1)
    flat_gates = gate_weights.reshape(-1)
    row_total = TOKENS * TOPK
    slot_total = TOKENS // ROWS_DEV * CAP

    def one_expert(carry_sum, expert):
        chosen = (flat_ids == expert).astype(jnp.int32)
        slot_index = jnp.cumsum(chosen) - chosen
        target = jnp.where(chosen > 0, slot_index, slot_total).astype(jnp.int32)
        owner = jnp.zeros((slot_total,), jnp.int32).at[target].set(jnp.arange(row_total, dtype=jnp.int32), mode='drop')
        filled = jnp.zeros((slot_total,), jnp.float32).at[target].set(1.0, mode='drop')
        token_index = owner // TOPK
        row_block_slice = normed[token_index]
        combined = jnp.zeros((slot_total, D), jnp.float32)
        for half_index in range(2):
            which = (2 * expert + half_index).astype(jnp.int32)
            gate_matrix = lax.dynamic_index_in_dim(w_gate, which, 0, keepdims=False)
            up_matrix = lax.dynamic_index_in_dim(w_up, which, 0, keepdims=False)
            down_matrix = lax.dynamic_index_in_dim(w_down, which, 0, keepdims=False)
            gate_act = jnp.dot(row_block_slice, gate_matrix, preferred_element_type=jnp.float32)
            up_act = jnp.dot(row_block_slice, up_matrix, preferred_element_type=jnp.float32)
            hidden = (jax.nn.silu(gate_act) * up_act).astype(jnp.bfloat16)
            part = jnp.dot(hidden, down_matrix, preferred_element_type=jnp.float32).astype(jnp.bfloat16)
            combined = combined + part.astype(jnp.float32)
        pair_output = lax.optimization_barrier(combined.astype(jnp.bfloat16)).astype(jnp.float32)
        scaled = pair_output * (flat_gates[owner] * filled)[:, None]
        return (carry_sum.at[token_index].add(scaled), None)
    expert_sum, ignored_slot = lax.scan(one_expert, jnp.zeros((TOKENS, D), jnp.float32), jnp.arange(EXPERTS, dtype=jnp.int32))
    return (mid + expert_sum).astype(jnp.bfloat16)
```

```python
import math

import jax
import jax.numpy as jnp
from jax import lax
from jax.sharding import Mesh, PartitionSpec as P

HQ = 32
KVH = 4
HD = 128
NX, NZ, NY, NC = 4, 8, 4, 2
ROWS = 64
CAP = 5
PLANE = NX * NY
SLOTS = NZ * CAP

BF = jnp.bfloat16
F32 = jnp.float32
masked_low = -1e30

RING = (0, -1, 1, -2, 2, -3, 3, 4)


def shift(value, axis, size, by):
    return lax.ppermute(value, axis, [(i, (i + by) % size) for i in range(size)])


def swap_cores(value):
    return lax.ppermute(value, "c", [(0, 1), (1, 0)])


def from_behind(value):
    devices = NX * NZ
    return lax.ppermute(value, ("x", "z"), [(i, i + 1) for i in range(devices - 1)])


def doc_of(positions, doc_lengths):
    doc_ends = jnp.cumsum(doc_lengths)
    return jnp.sum((positions[:, None] >= doc_ends[None, :]).astype(jnp.int32), axis=1)


def attend(queries, key_rows, value_rows, doc_lengths):
    tok_rows = queries.shape[0]
    half_rows = tok_rows // 2
    heads_here = queries.shape[1] // HD
    seq_index = lax.axis_index(("x", "z"))
    group_index = lax.axis_index("y")
    query_block_list = queries.reshape(2, half_rows, heads_here, HD)
    query_pos = seq_index * tok_rows + jnp.arange(tok_rows, dtype=jnp.int32)
    query_doc = doc_of(query_pos, doc_lengths).reshape(2, half_rows)
    query_pos = query_pos.reshape(2, half_rows)
    key_head = lax.dynamic_slice_in_dim(key_rows, group_index * HD, HD, 1)
    value_head = lax.dynamic_slice_in_dim(value_rows, group_index * HD, HD, 1)
    own_pair = jnp.stack([key_head, value_head])
    previous_tail = from_behind(own_pair[:, half_rows:])
    joined = jnp.concatenate([previous_tail, own_pair], axis=1)
    windows = jnp.stack([joined[:, :tok_rows], joined[:, half_rows:]], axis=1)
    key_pos = (
        seq_index * tok_rows
        - half_rows
        + jnp.arange(2, dtype=jnp.int32)[:, None] * half_rows
        + jnp.arange(tok_rows, dtype=jnp.int32)[None, :]
    )
    key_doc = doc_of(key_pos.reshape(-1), doc_lengths).reshape(2, tok_rows)
    scores = jnp.einsum(
        "fiza,fla->fzil", query_block_list, windows[0], preferred_element_type=F32
    ) * (1.0 / math.sqrt(HD))
    visible = (
        (key_pos[:, None, :] <= query_pos[:, :, None])
        & (key_doc[:, None, :] == query_doc[:, :, None])
        & (key_pos[:, None, :] >= 0)
    )
    visible = visible[:, None]
    row_top = jnp.max(jnp.where(visible, scores, masked_low), axis=3, keepdims=True)
    weights = jnp.exp(jnp.where(visible, scores - row_top, masked_low))
    totals = jnp.sum(weights, axis=3)
    mixture = jnp.einsum(
        "zvoe,zey->zvoy", weights.astype(BF), windows[1], preferred_element_type=F32
    )
    result = (mixture / totals[:, :, :, None]).astype(BF)
    return result.transpose(0, 2, 1, 3).reshape(tok_rows, heads_here * HD)


def project(attn_rows, out_weight):
    width = out_weight.shape[1]
    y, c = lax.axis_index("y"), lax.axis_index("c")
    blocks = attn_rows.reshape(NY, NC, ROWS, -1)

    def rows_for(core):
        picked = [
            lax.dynamic_slice(blocks, ((y + k) % NY, core, 0, 0), (1, 1, ROWS, blocks.shape[3]))
            for k in range(NY)
        ]
        return jnp.concatenate(picked, axis=0).reshape(NY * ROWS, -1)

    theirs = jnp.dot(rows_for(1 - c), out_weight, preferred_element_type=F32).astype(BF)
    arrived = swap_cores(theirs)
    mine = jnp.dot(rows_for(c), out_weight, preferred_element_type=F32)
    both = (mine + arrived.astype(F32)).reshape(NY, ROWS, width)
    total = both[0]
    for k in range(1, NY):
        total = total + shift(both[k].astype(BF), "y", NY, k).astype(F32)
    return total


def ring_gather(own):
    width = own.shape[1]
    half = width // 2
    right = left = own
    blocks = [own]
    for _ in range(3):
        right = shift(right, "z", NZ, 1)
        left = shift(left, "z", NZ, -1)
        blocks += [right, left]
    a = shift(right[:, :half], "z", NZ, 1)
    b = shift(left[:, half:], "z", NZ, -1)
    blocks.append(jnp.concatenate([a, b], axis=1))
    return jnp.concatenate(blocks, axis=0)


def ring_sum(blocks):
    half = blocks[0].shape[1] // 2

    def add(a, b):
        return (a.astype(F32) + b.astype(F32)).astype(BF)

    a = shift(blocks[4][:, :half], "z", NZ, 1)
    b = shift(blocks[4][:, half:], "z", NZ, -1)
    right = jnp.concatenate([add(blocks[3][:, :half], a), blocks[3][:, half:]], axis=1)
    left = jnp.concatenate([blocks[-3][:, :half], add(blocks[-3][:, half:], b)], axis=1)
    for step in (2, 1):
        right = add(shift(right, "z", NZ, 1), blocks[step])
        left = add(shift(left, "z", NZ, -1), blocks[-step])
    right = shift(right, "z", NZ, 1)
    left = shift(left, "z", NZ, -1)
    return blocks[0].astype(F32) + right.astype(F32) + left.astype(F32)


def slots_of(expert_ids, gate_weights):
    z = lax.axis_index("z")
    own = jnp.concatenate([expert_ids.astype(F32), gate_weights], axis=1)
    everywhere = lax.all_gather(own, "z", axis=0, tiled=False)
    order = (z + jnp.array(RING, jnp.int32)) % NZ
    everywhere = jnp.take(everywhere, order, axis=0)
    top = expert_ids.shape[1]
    ids = everywhere[:, :, :top].astype(jnp.int32)
    gates = everywhere[:, :, top:]
    place = jnp.arange(PLANE, dtype=jnp.int32)
    experts = (place // NY * NZ + z) * NY + place % NY
    match = ids[None] == experts[:, None, None, None]
    named = jnp.any(match, axis=3)
    gate = jnp.sum(jnp.where(match, gates[None], 0.0), axis=3)
    before = jnp.triu(jnp.ones((ROWS, ROWS), BF), 1)
    rank = jnp.dot(
        named.astype(BF).reshape(PLANE * NZ, ROWS), before, preferred_element_type=F32
    ).reshape(PLANE, NZ, ROWS)
    slot = rank.astype(jnp.int32) + jnp.arange(NZ, dtype=jnp.int32)[None, :, None] * CAP
    slot = jnp.where(named, slot, -1).reshape(PLANE, 1, NZ * ROWS)
    hit = slot == jnp.arange(SLOTS, dtype=jnp.int32)[None, :, None]
    one_hot = hit.astype(BF).reshape(PLANE * SLOTS, NZ * ROWS)
    weighted = jnp.where(hit, gate.reshape(PLANE, 1, NZ * ROWS), 0.0).astype(BF)
    return one_hot, weighted.reshape(PLANE * SLOTS, NZ * ROWS)


def expert_rows(rows, w_gate, w_up, w_down):
    gate_act = jnp.dot(rows, w_gate, preferred_element_type=F32)
    up_act = jnp.dot(rows, w_up, preferred_element_type=F32)
    hidden = (jax.nn.silu(gate_act) * up_act).astype(BF)
    return jnp.dot(hidden, w_down, preferred_element_type=F32).astype(BF)


def exchange(rows):
    width = rows.shape[1]
    out = lax.all_to_all(
        rows.reshape(PLANE, SLOTS, width), ("x", "y"), split_axis=0, concat_axis=0, tiled=True
    )
    return out.reshape(PLANE * SLOTS, width)


def local(
    queries,
    key_rows,
    value_rows,
    doc_lengths,
    residual_in,
    out_weight,
    norm_gain,
    expert_ids,
    gate_weights,
    w_gate,
    w_up,
    w_down,
):
    one_hot, weighted = slots_of(expert_ids, gate_weights)
    attn_rows = attend(queries, key_rows, value_rows, doc_lengths)
    mid = residual_in.astype(F32) + project(attn_rows, out_weight)
    spread = jnp.mean(mid * mid, axis=1, keepdims=True)
    normed = (mid * lax.rsqrt(spread + 1e-06) * norm_gain[None, :]).astype(BF)

    tokens = ring_gather(normed)
    outgoing = jnp.dot(one_hot, tokens, preferred_element_type=F32).astype(BF)
    mine = exchange(outgoing)
    theirs = swap_cores(mine)
    part_mine = expert_rows(mine, w_gate[0], w_up[0], w_down[0])
    part_theirs = expert_rows(theirs, w_gate[0], w_up[0], w_down[0])
    other_half = swap_cores(part_theirs)
    pair_out = (part_mine.astype(F32) + other_half.astype(F32)).astype(BF)
    returned = exchange(pair_out)
    plane_sum = lax.dot_general(
        weighted, returned, (((0,), (0,)), ((), ())), preferred_element_type=F32
    ).astype(BF)
    blocks = plane_sum.reshape(NZ, ROWS, -1)
    expert_sum = ring_sum({offset: blocks[i] for i, offset in enumerate(RING)})
    return (mid + expert_sum).astype(BF)


def solution(mesh):
    mesh = Mesh(mesh.devices.reshape(NX, NZ, NY, NC), ("x", "z", "y", "c"))
    seq, head = ("x", "z"), ("y", "c")
    every = seq + head
    placed = (
        P(seq, head),
        P(seq, None),
        P(seq, None),
        P(),
        P(every, None),
        P(head, None),
        P(),
        P(every, None),
        P(every, None),
        P(every, None, None),
        P(every, None, None),
        P(every, None, None),
    )
    return jax.shard_map(
        local, mesh=mesh, in_specs=placed, out_specs=P(every, None), check_vma=False
    )
```

```python
import math

import jax
import jax.numpy as jnp
from jax import lax
from jax.experimental import pallas as pl
from jax.experimental.pallas import tpu as pltpu
from jax.sharding import Mesh, PartitionSpec as P

HQ = 32
KVH = 4
HD = 128
NX, NZ, NY, NC = 4, 8, 4, 2
ROWS = 64
CAP = 5
PLANE = NX * NY
SLOTS = NZ * CAP

BF = jnp.bfloat16
F32 = jnp.float32
masked_low = -1e30

RING = (0, -1, 1, -2, 2, -3, 3, 4)


def shift(value, axis, size, by):
    return lax.ppermute(value, axis, [(i, (i + by) % size) for i in range(size)])


def swap_cores(value):
    return lax.ppermute(value, "c", [(0, 1), (1, 0)])


def from_behind(value):
    devices = NX * NZ
    return lax.ppermute(value, ("x", "z"), [(i, i + 1) for i in range(devices - 1)])


def doc_of(positions, doc_lengths):
    doc_ends = jnp.cumsum(doc_lengths)
    return jnp.sum((positions[:, None] >= doc_ends[None, :]).astype(jnp.int32), axis=1)


def attend(queries, key_rows, value_rows, doc_lengths):
    tok_rows = queries.shape[0]
    half_rows = tok_rows // 2
    heads_here = queries.shape[1] // HD
    seq_index = lax.axis_index(("x", "z"))
    group_index = lax.axis_index("y")
    query_block_list = queries.reshape(2, half_rows, heads_here, HD)
    query_pos = seq_index * tok_rows + jnp.arange(tok_rows, dtype=jnp.int32)
    query_doc = doc_of(query_pos, doc_lengths).reshape(2, half_rows)
    query_pos = query_pos.reshape(2, half_rows)
    key_head = lax.dynamic_slice_in_dim(key_rows, group_index * HD, HD, 1)
    value_head = lax.dynamic_slice_in_dim(value_rows, group_index * HD, HD, 1)
    own_pair = jnp.stack([key_head, value_head])
    previous_tail = from_behind(own_pair[:, half_rows:])
    joined = jnp.concatenate([previous_tail, own_pair], axis=1)
    windows = jnp.stack([joined[:, :tok_rows], joined[:, half_rows:]], axis=1)
    key_pos = (
        seq_index * tok_rows
        - half_rows
        + jnp.arange(2, dtype=jnp.int32)[:, None] * half_rows
        + jnp.arange(tok_rows, dtype=jnp.int32)[None, :]
    )
    key_doc = doc_of(key_pos.reshape(-1), doc_lengths).reshape(2, tok_rows)
    scores = jnp.einsum(
        "fiza,fla->fzil", query_block_list, windows[0], preferred_element_type=F32
    ) * (1.0 / math.sqrt(HD))
    visible = (
        (key_pos[:, None, :] <= query_pos[:, :, None])
        & (key_doc[:, None, :] == query_doc[:, :, None])
        & (key_pos[:, None, :] >= 0)
    )
    visible = visible[:, None]
    row_top = jnp.max(jnp.where(visible, scores, masked_low), axis=3, keepdims=True)
    weights = jnp.exp(jnp.where(visible, scores - row_top, masked_low))
    totals = jnp.sum(weights, axis=3)
    mixture = jnp.einsum(
        "zvoe,zey->zvoy", weights.astype(BF), windows[1], preferred_element_type=F32
    )
    result = (mixture / totals[:, :, :, None]).astype(BF)
    return result.transpose(0, 2, 1, 3).reshape(tok_rows, heads_here * HD)


def project(attn_rows, out_weight):
    width = out_weight.shape[1]
    y, c = lax.axis_index("y"), lax.axis_index("c")
    blocks = attn_rows.reshape(NY, NC, ROWS, -1)

    def rows_for(core):
        picked = [
            lax.dynamic_slice(blocks, ((y + k) % NY, core, 0, 0), (1, 1, ROWS, blocks.shape[3]))
            for k in range(NY)
        ]
        return jnp.concatenate(picked, axis=0).reshape(NY * ROWS, -1)

    theirs = jnp.dot(rows_for(1 - c), out_weight, preferred_element_type=F32).astype(BF)
    arrived = swap_cores(theirs)
    mine = jnp.dot(rows_for(c), out_weight, preferred_element_type=F32)
    both = (mine + arrived.astype(F32)).reshape(NY, ROWS, width)
    total = both[0]
    for k in range(1, NY):
        total = total + shift(both[k].astype(BF), "y", NY, k).astype(F32)
    return total


def ring_gather(own):
    width = own.shape[1]
    half = width // 2
    right = left = own
    blocks = [own]
    for _ in range(3):
        right = shift(right, "z", NZ, 1)
        left = shift(left, "z", NZ, -1)
        blocks += [right, left]
    a = shift(right[:, :half], "z", NZ, 1)
    b = shift(left[:, half:], "z", NZ, -1)
    blocks.append(jnp.concatenate([a, b], axis=1))
    return jnp.concatenate(blocks, axis=0)


def ring_sum(blocks):
    half = blocks[0].shape[1] // 2

    def add(a, b):
        return (a.astype(F32) + b.astype(F32)).astype(BF)

    a = shift(blocks[4][:, :half], "z", NZ, 1)
    b = shift(blocks[4][:, half:], "z", NZ, -1)
    right = jnp.concatenate([add(blocks[3][:, :half], a), blocks[3][:, half:]], axis=1)
    left = jnp.concatenate([blocks[-3][:, :half], add(blocks[-3][:, half:], b)], axis=1)
    for step in (2, 1):
        right = add(shift(right, "z", NZ, 1), blocks[step])
        left = add(shift(left, "z", NZ, -1), blocks[-step])
    right = shift(right, "z", NZ, 1)
    left = shift(left, "z", NZ, -1)
    return blocks[0].astype(F32) + right.astype(F32) + left.astype(F32)


def across_planes(own):
    z = lax.axis_index("z")
    held = own[None]
    for bit in (1, 2, 4):
        other = lax.ppermute(held, "z", [(i, i ^ bit) for i in range(NZ)])
        held = jnp.concatenate([held, other], axis=0)
    order = z ^ ((z + jnp.array(RING, jnp.int32)) % NZ)
    return jnp.take(held, order, axis=0)


def slots_of(expert_ids, gate_weights):
    z = lax.axis_index("z")
    top = expert_ids.shape[1]
    everywhere = across_planes(
        jnp.concatenate([expert_ids.T.astype(F32), gate_weights.T], axis=0)
    )
    ids = everywhere[:, :top].astype(jnp.int32)
    gates = everywhere[:, top:]
    place = jnp.arange(PLANE, dtype=jnp.int32)
    experts = (place // NY * NZ + z) * NY + place % NY
    match = ids[None] == experts[:, None, None, None]
    named = jnp.any(match, axis=2)
    gate = jnp.sum(jnp.where(match, gates[None], 0.0), axis=2)
    before = jnp.triu(jnp.ones((ROWS, ROWS), BF), 1)
    rank = jnp.dot(
        named.astype(BF).reshape(PLANE * NZ, ROWS), before, preferred_element_type=F32
    ).reshape(PLANE, NZ, ROWS)
    slot = rank.astype(jnp.int32) + jnp.arange(NZ, dtype=jnp.int32)[None, :, None] * CAP
    slot = jnp.where(named, slot, -1).reshape(PLANE, 1, NZ * ROWS)
    hit = slot == jnp.arange(SLOTS, dtype=jnp.int32)[None, :, None]
    one_hot = hit.astype(BF).reshape(PLANE * SLOTS, NZ * ROWS)
    weighted = jnp.where(hit, gate.reshape(PLANE, 1, NZ * ROWS), 0.0).astype(BF)
    return one_hot, weighted.reshape(PLANE * SLOTS, NZ * ROWS)


def expert_body(rows_ref, g0, g1, u0, u1, d0, d1, out_ref, g_all, u_all, d_all, hidden, sems):
    half = g0.shape[2]
    copies = [
        pltpu.make_async_copy(g0.at[0], g_all.at[:, :half], sems.at[0]),
        pltpu.make_async_copy(g1.at[0], g_all.at[:, half:], sems.at[1]),
        pltpu.make_async_copy(u0.at[0], u_all.at[:, :half], sems.at[2]),
        pltpu.make_async_copy(u1.at[0], u_all.at[:, half:], sems.at[3]),
        pltpu.make_async_copy(d0.at[0], d_all.at[:half], sems.at[4]),
        pltpu.make_async_copy(d1.at[0], d_all.at[half:], sems.at[5]),
    ]
    for copy in copies:
        copy.start()
    tile = 256
    for copy in copies[:4]:
        copy.wait()

    def inner(i, carry):
        at = pl.ds(pl.multiple_of(i * tile, tile), tile)
        gate_act = jnp.dot(rows_ref[...], g_all[:, at], preferred_element_type=F32)
        up_act = jnp.dot(rows_ref[...], u_all[:, at], preferred_element_type=F32)
        hidden[:, at] = (gate_act / (1.0 + jnp.exp(-gate_act)) * up_act).astype(BF)
        return carry

    lax.fori_loop(0, g_all.shape[1] // tile, inner, 0)
    for copy in copies[4:]:
        copy.wait()

    def outer(i, carry):
        at = pl.ds(pl.multiple_of(i * tile, tile), tile)
        out_ref[:, at] = jnp.dot(
            hidden[...], d_all[:, at], preferred_element_type=F32
        ).astype(BF)
        return carry

    lax.fori_loop(0, d_all.shape[1] // tile, outer, 0)


def expert_rows(rows, gate_pair, up_pair, down_pair):
    count, width = rows.shape
    hid = 2 * gate_pair[0].shape[2]
    whole = pl.BlockSpec(memory_space=pltpu.VMEM)
    there = pl.BlockSpec(memory_space=pltpu.HBM)
    return pl.pallas_call(
        expert_body,
        out_shape=jax.ShapeDtypeStruct((count, width), BF),
        in_specs=[whole] + [there] * 6,
        out_specs=whole,
        scratch_shapes=[
            pltpu.VMEM((width, hid), BF),
            pltpu.VMEM((width, hid), BF),
            pltpu.VMEM((hid, width), BF),
            pltpu.VMEM((count, hid), BF),
            pltpu.SemaphoreType.DMA((6,)),
        ],
        compiler_params=pltpu.CompilerParams(vmem_limit_bytes=28 * 1024 * 1024),
        cost_estimate=pl.CostEstimate(
            flops=6 * count * width * hid,
            bytes_accessed=6 * width * hid + 4 * count * width,
            transcendentals=count * hid,
        ),
    )(rows, *gate_pair, *up_pair, *down_pair)


def exchange(rows):
    width = rows.shape[1]
    out = lax.all_to_all(
        rows.reshape(PLANE, SLOTS, width), ("x", "y"), split_axis=0, concat_axis=0, tiled=True
    )
    return out.reshape(PLANE * SLOTS, width)


def local(
    queries,
    key_rows,
    value_rows,
    doc_lengths,
    residual_in,
    out_weight,
    norm_gain,
    expert_ids,
    gate_weights,
    w_gate,
    w_up,
    w_down,
):
    pairs = [(w, swap_cores(w)) for w in (w_gate, w_up, w_down)]
    one_hot, weighted = slots_of(expert_ids, gate_weights)
    attn_rows = attend(queries, key_rows, value_rows, doc_lengths)
    mid = residual_in.astype(F32) + project(attn_rows, out_weight)
    spread = jnp.mean(mid * mid, axis=1, keepdims=True)
    normed = (mid * lax.rsqrt(spread + 1e-06) * norm_gain[None, :]).astype(BF)

    normed, pairs, one_hot, weighted = lax.optimization_barrier(
        (normed, pairs, one_hot, weighted)
    )
    tokens = ring_gather(normed)
    outgoing = jnp.dot(one_hot, tokens, preferred_element_type=F32).astype(BF)
    mine = exchange(outgoing)
    pair_out = expert_rows(mine, *pairs)
    returned = exchange(pair_out)
    plane_sum = lax.dot_general(
        weighted, returned, (((0,), (0,)), ((), ())), preferred_element_type=F32
    ).astype(BF)
    blocks = plane_sum.reshape(NZ, ROWS, -1)
    expert_sum = ring_sum({offset: blocks[i] for i, offset in enumerate(RING)})
    return (mid + expert_sum).astype(BF)


def solution(mesh):
    mesh = Mesh(mesh.devices.reshape(NX, NZ, NY, NC), ("x", "z", "y", "c"))
    seq, head = ("x", "z"), ("y", "c")
    every = seq + head
    placed = (
        P(seq, head),
        P(seq, None),
        P(seq, None),
        P(),
        P(every, None),
        P(head, None),
        P(),
        P(every, None),
        P(every, None),
        P(every, None, None),
        P(every, None, None),
        P(every, None, None),
    )
    return jax.shard_map(
        local, mesh=mesh, in_specs=placed, out_specs=P(every, None), check_vma=False
    )
```

```python
import math

import jax
import jax.numpy as jnp
from jax import lax
from jax.experimental import pallas as pl
from jax.experimental.pallas import tpu as pltpu
from jax.sharding import Mesh, PartitionSpec as P

HD = 128
NDOCS = 128
NX, NZ, NY, NC = 4, 8, 4, 2
ROWS = 64
CAP = 5
PLANE = NX * NY
SLOTS = NZ * CAP

BF = jnp.bfloat16
F32 = jnp.float32
masked_low = -1e30

RING = (0, -1, 1, -2, 2, -3, 3, 4)


def shift(value, axis, size, by):
    return lax.ppermute(value, axis, [(i, (i + by) % size) for i in range(size)])


def swap_cores(value):
    return lax.ppermute(value, "c", [(0, 1), (1, 0)])


def from_behind(value):
    devices = NX * NZ
    return lax.ppermute(value, ("x", "z"), [(i, i + 1) for i in range(devices - 1)])


def attend_half(base, queries, keys, values, lengths, store):
    rows = queries.shape[0]
    place = lax.broadcasted_iota(jnp.int32, (NDOCS, NDOCS), 0)
    upto = place <= lax.broadcasted_iota(jnp.int32, (NDOCS, NDOCS), 1)
    spread = jnp.broadcast_to(lengths.astype(F32), (8, NDOCS)).astype(BF)
    ends = jnp.dot(spread, jnp.where(upto, 1.0, 0.0).astype(BF), preferred_element_type=F32)[:1]
    query_pos = base + lax.broadcasted_iota(jnp.int32, (rows, 1), 0)
    ended = ends <= query_pos.astype(F32)
    start = jnp.max(jnp.where(ended, ends, 0.0), axis=1, keepdims=True).astype(jnp.int32)
    span = 2 * keys[0].shape[0]
    key_pos = base - keys[0].shape[0] + lax.broadcasted_iota(jnp.int32, (1, span), 1)
    visible = (key_pos <= query_pos) & (key_pos >= start)
    key_window = jnp.concatenate(keys, axis=0)
    value_window = jnp.concatenate(values, axis=0)
    for head in range(queries.shape[1] // HD):
        at = slice(head * HD, (head + 1) * HD)
        scores = lax.dot_general(
            queries[:, at], key_window, (((1,), (1,)), ((), ())), preferred_element_type=F32
        ) * (1.0 / math.sqrt(HD))
        scores = jnp.where(visible, scores, masked_low)
        weights = jnp.exp(scores - jnp.max(scores, axis=1, keepdims=True))
        total = jnp.sum(weights, axis=1, keepdims=True)
        mixture = jnp.dot(weights.astype(BF), value_window, preferred_element_type=F32)
        store(at, (mixture / total).astype(BF))


def late_body(where, q_ref, ka, kb, va, vb, len_ref, out_ref):
    def store(at, value):
        out_ref[:, at] = value

    attend_half(
        where[0] + q_ref.shape[0], q_ref[...], [ka[...], kb[...]], [va[...], vb[...]], len_ref[...], store
    )


def early_body(
    where, q_ref, tails, kb, vb, len_ref, late_ref, w_ref, theirs_ref, mine_ref, held, picked
):
    rows = q_ref.shape[0]

    def store(at, value):
        held[:rows, at] = value

    held[rows:] = late_ref[...]
    attend_half(
        where[0], q_ref[...], [tails[0], kb[...]], [tails[1], vb[...]], len_ref[...], store
    )
    y, c = where[1], where[2]
    for k in range(NY):
        block = lax.rem(y + k, NY) * (NC * ROWS)
        here = pl.ds(pl.multiple_of(block + c * ROWS, ROWS), ROWS)
        there = pl.ds(pl.multiple_of(block + (1 - c) * ROWS, ROWS), ROWS)
        mine_ref[k * ROWS : (k + 1) * ROWS] = held[here]
        picked[k * ROWS : (k + 1) * ROWS] = held[there]
    tile = 512

    def column(i, carry):
        at = pl.ds(pl.multiple_of(i * tile, tile), tile)
        theirs_ref[:, at] = jnp.dot(
            picked[...], w_ref[:, at], preferred_element_type=F32
        ).astype(BF)
        return carry

    lax.fori_loop(0, w_ref.shape[1] // tile, column, 0)


def attend(queries, key_rows, value_rows, doc_lengths, out_weight, held):
    tok_rows, width = queries.shape
    half = tok_rows // 2
    out_width = out_weight.shape[1]
    y, c = lax.axis_index("y"), lax.axis_index("c")
    where = jnp.stack([lax.axis_index(("x", "z")) * tok_rows, y, c]).astype(jnp.int32)
    lengths = doc_lengths.reshape(1, -1)
    tails = from_behind(
        jnp.stack(
            [
                lax.dynamic_slice(rows, (half, y * HD), (half, HD))
                for rows in (key_rows, value_rows)
            ]
        )
    )

    def part(i):
        return pl.BlockSpec((half, HD), lambda g, where: (i, where[1]))

    def all_of(*shape):
        return pl.BlockSpec(shape, lambda g, where: (0,) * len(shape))

    lens = all_of(1, doc_lengths.shape[0])
    params = pltpu.CompilerParams(vmem_limit_bytes=56 * 1024 * 1024)
    scores = tok_rows * tok_rows * (width // HD) // 2
    late = pl.pallas_call(
        late_body,
        out_shape=jax.ShapeDtypeStruct((half, width), BF),
        grid_spec=pltpu.PrefetchScalarGridSpec(
            num_scalar_prefetch=1,
            grid=(1,),
            in_specs=[
                pl.BlockSpec((half, width), lambda g, where: (1, 0)),
                part(0),
                part(1),
                part(0),
                part(1),
                lens,
            ],
            out_specs=all_of(half, width),
        ),
        compiler_params=params,
        cost_estimate=pl.CostEstimate(
            flops=16 * scores * HD, bytes_accessed=6 * half * width, transcendentals=8 * scores
        ),
    )(where, queries, key_rows, key_rows, value_rows, value_rows, lengths)
    late, held = lax.optimization_barrier((late, double(held, 1)))
    theirs, mine = pl.pallas_call(
        early_body,
        out_shape=(
            jax.ShapeDtypeStruct((half, out_width), BF),
            jax.ShapeDtypeStruct((half, width), BF),
        ),
        grid_spec=pltpu.PrefetchScalarGridSpec(
            num_scalar_prefetch=1,
            grid=(1,),
            in_specs=[
                pl.BlockSpec((half, width), lambda g, where: (0, 0)),
                all_of(2, half, HD),
                part(0),
                part(0),
                lens,
                all_of(half, width),
                all_of(*out_weight.shape),
            ],
            out_specs=(all_of(half, out_width), all_of(half, width)),
            scratch_shapes=[pltpu.VMEM((tok_rows, width), BF), pltpu.VMEM((half, width), BF)],
        ),
        compiler_params=params,
        cost_estimate=pl.CostEstimate(
            flops=16 * scores * HD + 2 * half * width * out_width,
            bytes_accessed=6 * half * width + 2 * width * out_width,
            transcendentals=8 * scores,
        ),
    )(where, queries, tails, key_rows, value_rows, lengths, late, out_weight)
    theirs, held = lax.optimization_barrier((theirs, double(held, 2)))
    return theirs, mine, held


def project(theirs, attn_mine, out_weight, held):
    arrived, held = lax.optimization_barrier((swap_cores(theirs), double(held, 4)))
    mine = lax.optimization_barrier(
        jnp.dot(attn_mine, out_weight, preferred_element_type=F32)
    )
    both = (mine + arrived.astype(F32)).reshape(NY, ROWS, out_weight.shape[1])
    sent = both.astype(BF)
    moved = [shift(sent[k], "y", NY, k) for k in range(1, NY)]
    return both[0] + sum(block.astype(F32) for block in moved), held


def ring_gather(own):
    width = own.shape[1]
    half = width // 2
    right = left = own
    blocks = [own]
    for _ in range(3):
        right = shift(right, "z", NZ, 1)
        left = shift(left, "z", NZ, -1)
        blocks += [right, left]
    a = shift(right[:, :half], "z", NZ, 1)
    b = shift(left[:, half:], "z", NZ, -1)
    blocks.append(jnp.concatenate([a, b], axis=1))
    return jnp.concatenate(blocks, axis=0)


def ring_sum(blocks):
    half = blocks[0].shape[1] // 2

    def add(a, b):
        return (a.astype(F32) + b.astype(F32)).astype(BF)

    a = shift(blocks[4][:, :half], "z", NZ, 1)
    b = shift(blocks[4][:, half:], "z", NZ, -1)
    right = jnp.concatenate([add(blocks[3][:, :half], a), blocks[3][:, half:]], axis=1)
    left = jnp.concatenate([blocks[-3][:, :half], add(blocks[-3][:, half:], b)], axis=1)
    right, left = lax.optimization_barrier(right), lax.optimization_barrier(left)
    for step in (2, 1):
        right = lax.optimization_barrier(add(shift(right, "z", NZ, 1), blocks[step]))
        left = lax.optimization_barrier(add(shift(left, "z", NZ, -1), blocks[-step]))
    right = shift(right, "z", NZ, 1)
    left = shift(left, "z", NZ, -1)
    return blocks[0].astype(F32) + right.astype(F32) + left.astype(F32)


def double(held, bit):
    other = lax.ppermute(held, "z", [(i, i ^ bit) for i in range(NZ)])
    return jnp.concatenate([held, other], axis=0)


def slots_of(held):
    z = lax.axis_index("z")
    order = z ^ ((z + jnp.array(RING, jnp.int32)) % NZ)
    everywhere = jnp.take(held, order, axis=0)
    top = held.shape[1] // 2
    ids = everywhere[:, :top].astype(jnp.int32)
    gates = everywhere[:, top:]
    place = jnp.arange(PLANE, dtype=jnp.int32)
    experts = (place // NY * NZ + z) * NY + place % NY
    match = ids[None] == experts[:, None, None, None]
    named = jnp.any(match, axis=2)
    gate = jnp.sum(jnp.where(match, gates[None], 0.0), axis=2)
    before = jnp.triu(jnp.ones((ROWS, ROWS), BF), 1)
    rank = jnp.dot(
        named.astype(BF).reshape(PLANE * NZ, ROWS), before, preferred_element_type=F32
    ).reshape(PLANE, NZ, ROWS)
    slot = rank.astype(jnp.int32) + jnp.arange(NZ, dtype=jnp.int32)[None, :, None] * CAP
    slot = jnp.where(named, slot, -1).reshape(PLANE, 1, NZ * ROWS)
    hit = slot == jnp.arange(SLOTS, dtype=jnp.int32)[None, :, None]
    one_hot = hit.astype(BF).reshape(PLANE * SLOTS, NZ * ROWS)
    weighted = jnp.where(hit, gate.reshape(PLANE, 1, NZ * ROWS), 0.0).astype(BF)
    return one_hot, weighted.reshape(PLANE * SLOTS, NZ * ROWS)


def expert_body(rows_ref, g0, g1, u0, u1, d0, d1, out_ref, g_all, u_all, d_all, hidden, sems):
    half = g0.shape[2]
    copies = [
        pltpu.make_async_copy(g0.at[0], g_all.at[:, :half], sems.at[0]),
        pltpu.make_async_copy(g1.at[0], g_all.at[:, half:], sems.at[1]),
        pltpu.make_async_copy(u0.at[0], u_all.at[:, :half], sems.at[2]),
        pltpu.make_async_copy(u1.at[0], u_all.at[:, half:], sems.at[3]),
        pltpu.make_async_copy(d0.at[0], d_all.at[:half], sems.at[4]),
        pltpu.make_async_copy(d1.at[0], d_all.at[half:], sems.at[5]),
    ]
    for which in (0, 2, 1, 3, 4, 5):
        copies[which].start()
    tile = 256
    for i in range(g_all.shape[1] // tile):
        if i == 0:
            copies[0].wait()
            copies[2].wait()
        if i == half // tile:
            copies[1].wait()
            copies[3].wait()
        at = slice(i * tile, (i + 1) * tile)
        gate_act = jnp.dot(rows_ref[...], g_all[:, at], preferred_element_type=F32)
        up_act = jnp.dot(rows_ref[...], u_all[:, at], preferred_element_type=F32)
        hidden[:, at] = (gate_act / (1.0 + jnp.exp(-gate_act)) * up_act).astype(BF)
    for copy in copies[4:]:
        copy.wait()

    def outer(i, carry):
        at = pl.ds(pl.multiple_of(i * tile, tile), tile)
        out_ref[:, at] = jnp.dot(
            hidden[...], d_all[:, at], preferred_element_type=F32
        ).astype(BF)
        return carry

    lax.fori_loop(0, d_all.shape[1] // tile, outer, 0)


def expert_rows(rows, gate_pair, up_pair, down_pair):
    count, width = rows.shape
    hid = 2 * gate_pair[0].shape[2]
    whole = pl.BlockSpec(memory_space=pltpu.VMEM)
    there = pl.BlockSpec(memory_space=pltpu.HBM)
    return pl.pallas_call(
        expert_body,
        out_shape=jax.ShapeDtypeStruct((count, width), BF),
        in_specs=[whole] + [there] * 6,
        out_specs=whole,
        scratch_shapes=[
            pltpu.VMEM((width, hid), BF),
            pltpu.VMEM((width, hid), BF),
            pltpu.VMEM((hid, width), BF),
            pltpu.VMEM((count, hid), BF),
            pltpu.SemaphoreType.DMA((6,)),
        ],
        compiler_params=pltpu.CompilerParams(vmem_limit_bytes=28 * 1024 * 1024),
        cost_estimate=pl.CostEstimate(
            flops=6 * count * width * hid,
            bytes_accessed=6 * width * hid + 4 * count * width,
            transcendentals=count * hid,
        ),
    )(rows, *gate_pair, *up_pair, *down_pair)


def exchange(rows):
    width = rows.shape[1]
    out = lax.all_to_all(
        rows.reshape(PLANE, SLOTS, width), ("x", "y"), split_axis=0, concat_axis=0, tiled=True
    )
    return out.reshape(PLANE * SLOTS, width)


def local(
    queries,
    key_rows,
    value_rows,
    doc_lengths,
    residual_in,
    out_weight,
    norm_gain,
    expert_ids,
    gate_weights,
    w_gate,
    w_up,
    w_down,
):
    pairs = [(w, swap_cores(w)) for w in (w_gate, w_up, w_down)]
    held = jnp.concatenate([expert_ids.T.astype(F32), gate_weights.T], axis=0)[None]
    theirs, attn_mine, held = attend(
        queries, key_rows, value_rows, doc_lengths, out_weight, held
    )
    projected, held = project(theirs, attn_mine, out_weight, held)
    mid = residual_in.astype(F32) + projected
    one_hot, weighted = slots_of(held)
    spread = jnp.mean(mid * mid, axis=1, keepdims=True)
    normed = (mid * lax.rsqrt(spread + 1e-06) * norm_gain[None, :]).astype(BF)

    tokens, one_hot, weighted, pairs = lax.optimization_barrier(
        (ring_gather(normed), one_hot, weighted, pairs)
    )
    outgoing = jnp.dot(one_hot, tokens, preferred_element_type=F32).astype(BF)
    mine = exchange(outgoing)
    pair_out = expert_rows(mine, *pairs)
    returned = exchange(pair_out)
    plane_sum = lax.dot_general(
        weighted, returned, (((0,), (0,)), ((), ())), preferred_element_type=F32
    ).astype(BF)
    blocks = plane_sum.reshape(NZ, ROWS, -1)
    expert_sum = ring_sum({offset: blocks[i] for i, offset in enumerate(RING)})
    return (mid + expert_sum).astype(BF)


def solution(mesh):
    mesh = Mesh(mesh.devices.reshape(NX, NZ, NY, NC), ("x", "z", "y", "c"))
    seq, head = ("x", "z"), ("y", "c")
    every = seq + head
    placed = (
        P(seq, head),
        P(seq, None),
        P(seq, None),
        P(),
        P(every, None),
        P(head, None),
        P(),
        P(every, None),
        P(every, None),
        P(every, None, None),
        P(every, None, None),
        P(every, None, None),
    )
    return jax.shard_map(
        local, mesh=mesh, in_specs=placed, out_specs=P(every, None), check_vma=False
    )
```

```python
import math

import jax
import jax.numpy as jnp
from jax import lax
from jax.experimental import pallas as pl
from jax.experimental.pallas import tpu as pltpu
from jax.sharding import Mesh, PartitionSpec as P

HD = 128
NDOCS = 128
NX, NZ, NY, NC = 4, 8, 4, 2
ROWS = 64
CAP = 5
TOP = 8
META = 128
PLANE = NX * NY
SLOTS = NZ * CAP

BF = jnp.bfloat16
F32 = jnp.float32
masked_low = -1e30

RING = (0, -1, 1, -2, 2, -3, 3, 4)


def shift(value, axis, size, by):
    return lax.ppermute(value, axis, [(i, (i + by) % size) for i in range(size)])


def swap_cores(value):
    return lax.ppermute(value, "c", [(0, 1), (1, 0)])


def from_behind(value):
    devices = NX * NZ
    return lax.ppermute(value, ("x", "z"), [(i, i + 1) for i in range(devices - 1)])


def attend_half(base, queries, keys, values, lengths, store):
    rows = queries.shape[0]
    place = lax.broadcasted_iota(jnp.int32, (NDOCS, NDOCS), 0)
    upto = place <= lax.broadcasted_iota(jnp.int32, (NDOCS, NDOCS), 1)
    spread = jnp.broadcast_to(lengths.astype(F32), (8, NDOCS)).astype(BF)
    ends = jnp.dot(spread, jnp.where(upto, 1.0, 0.0).astype(BF), preferred_element_type=F32)[:1]
    query_pos = base + lax.broadcasted_iota(jnp.int32, (rows, 1), 0)
    ended = ends <= query_pos.astype(F32)
    start = jnp.max(jnp.where(ended, ends, 0.0), axis=1, keepdims=True).astype(jnp.int32)
    span = 2 * keys[0].shape[0]
    key_pos = base - keys[0].shape[0] + lax.broadcasted_iota(jnp.int32, (1, span), 1)
    visible = (key_pos <= query_pos) & (key_pos >= start)
    key_window = jnp.concatenate(keys, axis=0)
    value_window = jnp.concatenate(values, axis=0)
    for head in range(queries.shape[1] // HD):
        at = slice(head * HD, (head + 1) * HD)
        scores = lax.dot_general(
            queries[:, at], key_window, (((1,), (1,)), ((), ())), preferred_element_type=F32
        ) * (1.0 / math.sqrt(HD))
        scores = jnp.where(visible, scores, masked_low)
        weights = jnp.exp(scores - jnp.max(scores, axis=1, keepdims=True))
        total = jnp.sum(weights, axis=1, keepdims=True)
        mixture = jnp.dot(weights.astype(BF), value_window, preferred_element_type=F32)
        store(at, (mixture / total).astype(BF))


def late_body(where, q_ref, ka, kb, va, vb, len_ref, out_ref):
    def store(at, value):
        out_ref[:, at] = value

    attend_half(
        where[0] + q_ref.shape[0], q_ref[...], [ka[...], kb[...]], [va[...], vb[...]], len_ref[...], store
    )


def early_body(where, q_ref, tails, kb, vb, len_ref, late_ref, theirs_ref, mine_ref, held):
    rows = q_ref.shape[0]

    def store(at, value):
        held[:rows, at] = value

    held[rows:] = late_ref[...]
    attend_half(
        where[0], q_ref[...], [tails[0], kb[...]], [tails[1], vb[...]], len_ref[...], store
    )
    y, c = where[1], where[2]
    for k in range(NY):
        block = lax.rem(y + k, NY) * (NC * ROWS)
        here = pl.ds(pl.multiple_of(block + c * ROWS, ROWS), ROWS)
        there = pl.ds(pl.multiple_of(block + (1 - c) * ROWS, ROWS), ROWS)
        mine_ref[k * ROWS : (k + 1) * ROWS] = held[here]
        theirs_ref[k * ROWS : (k + 1) * ROWS] = held[there]


def attend(queries, key_rows, value_rows, doc_lengths):
    tok_rows, width = queries.shape
    half = tok_rows // 2
    y, c = lax.axis_index("y"), lax.axis_index("c")
    where = jnp.stack([lax.axis_index(("x", "z")) * tok_rows, y, c]).astype(jnp.int32)
    lengths = doc_lengths.reshape(1, -1)
    tails = from_behind(
        jnp.stack(
            [
                lax.dynamic_slice(rows, (half, y * HD), (half, HD))
                for rows in (key_rows, value_rows)
            ]
        )
    )

    def part(i):
        return pl.BlockSpec((half, HD), lambda g, where: (i, where[1]))

    def all_of(*shape):
        return pl.BlockSpec(shape, lambda g, where: (0,) * len(shape))

    lens = all_of(1, doc_lengths.shape[0])
    params = pltpu.CompilerParams(vmem_limit_bytes=57 * 1024 * 1024)
    scores = tok_rows * tok_rows * (width // HD) // 2
    late = pl.pallas_call(
        late_body,
        out_shape=jax.ShapeDtypeStruct((half, width), BF),
        grid_spec=pltpu.PrefetchScalarGridSpec(
            num_scalar_prefetch=1,
            grid=(1,),
            in_specs=[
                pl.BlockSpec((half, width), lambda g, where: (1, 0)),
                part(0),
                part(1),
                part(0),
                part(1),
                lens,
            ],
            out_specs=all_of(half, width),
        ),
        compiler_params=params,
        cost_estimate=pl.CostEstimate(
            flops=16 * scores * HD, bytes_accessed=6 * half * width, transcendentals=8 * scores
        ),
    )(where, queries, key_rows, key_rows, value_rows, value_rows, lengths)
    return pl.pallas_call(
        early_body,
        out_shape=(
            jax.ShapeDtypeStruct((half, width), BF),
            jax.ShapeDtypeStruct((half, width), BF),
        ),
        grid_spec=pltpu.PrefetchScalarGridSpec(
            num_scalar_prefetch=1,
            grid=(1,),
            in_specs=[
                pl.BlockSpec((half, width), lambda g, where: (0, 0)),
                all_of(2, half, HD),
                part(0),
                part(0),
                lens,
                all_of(half, width),
            ],
            out_specs=(all_of(half, width), all_of(half, width)),
            scratch_shapes=[pltpu.VMEM((tok_rows, width), BF)],
        ),
        compiler_params=params,
        cost_estimate=pl.CostEstimate(
            flops=16 * scores * HD, bytes_accessed=8 * half * width, transcendentals=8 * scores
        ),
    )(where, queries, tails, key_rows, value_rows, lengths, late)


def project(attn_theirs, attn_mine, out_weight):
    theirs = jnp.dot(attn_theirs, out_weight, preferred_element_type=F32).astype(BF)
    arrived = swap_cores(theirs)
    mine = lax.optimization_barrier(
        jnp.dot(attn_mine, out_weight, preferred_element_type=F32)
    )
    both = (mine + arrived.astype(F32)).reshape(NY, ROWS, out_weight.shape[1])
    sent = both.astype(BF)
    moved = [shift(sent[k], "y", NY, k) for k in range(1, NY)]
    return both[0] + sum(block.astype(F32) for block in moved)


def ring_gather(own, half):
    right = left = own
    blocks = [own]
    for _ in range(3):
        right = shift(right, "z", NZ, 1)
        left = shift(left, "z", NZ, -1)
        blocks += [right, left]
    return blocks + [shift(right[:, :half], "z", NZ, 1), shift(left[:, half:], "z", NZ, -1)]


def ring_sum(blocks):
    half = blocks[0].shape[1] // 2

    def add(a, b):
        return (a.astype(F32) + b.astype(F32)).astype(BF)

    a = shift(blocks[4][:, :half], "z", NZ, 1)
    b = shift(blocks[4][:, half:], "z", NZ, -1)
    right = jnp.concatenate([add(blocks[3][:, :half], a), blocks[3][:, half:]], axis=1)
    left = jnp.concatenate([blocks[-3][:, :half], add(blocks[-3][:, half:], b)], axis=1)
    for step in (2, 1):
        right = add(shift(right, "z", NZ, 1), blocks[step])
        own = lax.optimization_barrier((blocks[-step], right))[0]
        left = add(shift(left, "z", NZ, -1), own)
    right = shift(right, "z", NZ, 1)
    left = shift(left, "z", NZ, -1)
    return blocks[0].astype(F32) + right.astype(F32) + left.astype(F32)


def dispatch_body(z_ref, *refs):
    blocks, (out_ref, weight_ref, tokens, meta, one_hot) = refs[:-5], refs[-5:]
    width = tokens.shape[1]
    count = tokens.shape[0]
    cut = blocks[-2].shape[1]
    for i, block in enumerate(blocks[:-2]):
        at = slice(i * ROWS, (i + 1) * ROWS)
        tokens[at] = block[:, :width]
        meta[at] = block[:, width:]
    at = slice(count - ROWS, count)
    tokens[at, :cut] = blocks[-2][...]
    tokens[at, cut:] = blocks[-1][:, : width - cut]
    meta[at] = blocks[-1][:, width - cut :]

    turned = meta[...].astype(F32).T
    ids, gates = turned[:TOP], turned[TOP : 2 * TOP]
    named, gate = [], []
    for place in range(PLANE):
        expert = (place // NY * NZ + z_ref[0]) * NY + place % NY
        match = ids == expert.astype(F32)
        named.append(jnp.max(jnp.where(match, 1.0, 0.0), axis=0, keepdims=True))
        gate.append(jnp.sum(jnp.where(match, gates, 0.0), axis=0, keepdims=True))
    first = lax.broadcasted_iota(jnp.int32, (count, count), 0)
    second = lax.broadcasted_iota(jnp.int32, (count, count), 1)
    before = (first < second) & (first // ROWS == second // ROWS)
    all_named = jnp.concatenate(named, axis=0)
    rank = jnp.dot(
        all_named.astype(BF), jnp.where(before, 1.0, 0.0).astype(BF), preferred_element_type=F32
    )
    block_start = lax.broadcasted_iota(jnp.int32, (1, count), 1) // ROWS * CAP
    slot = jnp.where(all_named > 0.0, rank + block_start.astype(F32), -1.0)
    slots = lax.broadcasted_iota(jnp.int32, (SLOTS, 1), 0).astype(F32)
    for pair in range(PLANE // 2):
        hits, weights = [], []
        for place in (2 * pair, 2 * pair + 1):
            hit = slot[place : place + 1] == slots
            hits.append(jnp.where(hit, 1.0, 0.0))
            weights.append(jnp.where(hit, gate[place], 0.0))
        at = slice(2 * pair * SLOTS, (2 * pair + 2) * SLOTS)
        one_hot[at] = jnp.concatenate(hits, axis=0).astype(BF)
        weight_ref[at] = jnp.concatenate(weights, axis=0).astype(BF)
    tile = 256

    def column(i, carry):
        at = pl.ds(pl.multiple_of(i * tile, tile), tile)
        out_ref[:, at] = jnp.dot(
            one_hot[...], tokens[:, at], preferred_element_type=F32
        ).astype(BF)
        return carry

    lax.fori_loop(0, width // tile, column, 0)


def dispatch(blocks, width):
    count = NZ * ROWS
    whole = pl.BlockSpec(memory_space=pltpu.VMEM)
    return pl.pallas_call(
        dispatch_body,
        out_shape=(
            jax.ShapeDtypeStruct((PLANE * SLOTS, width), BF),
            jax.ShapeDtypeStruct((PLANE * SLOTS, count), BF),
        ),
        in_specs=[pl.BlockSpec(memory_space=pltpu.SMEM)] + [whole] * len(blocks),
        out_specs=(whole, whole),
        scratch_shapes=[
            pltpu.VMEM((count, width), BF),
            pltpu.VMEM((count, META), BF),
            pltpu.VMEM((PLANE * SLOTS, count), BF),
        ],
        compiler_params=pltpu.CompilerParams(vmem_limit_bytes=24 * 1024 * 1024),
        cost_estimate=pl.CostEstimate(
            flops=2 * PLANE * SLOTS * count * width,
            bytes_accessed=4 * count * width,
            transcendentals=0,
        ),
    )(lax.axis_index("z").astype(jnp.int32).reshape(1), *blocks)


def expert_body(rows_ref, g0, g1, u0, u1, d0, d1, out_ref, g_all, u_all, d_all, hidden, sems):
    half = g0.shape[2]
    copies = [
        pltpu.make_async_copy(g0.at[0], g_all.at[:, :half], sems.at[0]),
        pltpu.make_async_copy(g1.at[0], g_all.at[:, half:], sems.at[1]),
        pltpu.make_async_copy(u0.at[0], u_all.at[:, :half], sems.at[2]),
        pltpu.make_async_copy(u1.at[0], u_all.at[:, half:], sems.at[3]),
        pltpu.make_async_copy(d0.at[0], d_all.at[:half], sems.at[4]),
        pltpu.make_async_copy(d1.at[0], d_all.at[half:], sems.at[5]),
    ]
    for which in (0, 2, 1, 3, 4, 5):
        copies[which].start()
    tile = 256
    for i in range(g_all.shape[1] // tile):
        if i == 0:
            copies[0].wait()
            copies[2].wait()
        if i == half // tile:
            copies[1].wait()
            copies[3].wait()
        at = slice(i * tile, (i + 1) * tile)
        gate_act = jnp.dot(rows_ref[...], g_all[:, at], preferred_element_type=F32)
        up_act = jnp.dot(rows_ref[...], u_all[:, at], preferred_element_type=F32)
        hidden[:, at] = (gate_act / (1.0 + jnp.exp(-gate_act)) * up_act).astype(BF)
    for copy in copies[4:]:
        copy.wait()

    def outer(i, carry):
        at = pl.ds(pl.multiple_of(i * tile, tile), tile)
        out_ref[:, at] = jnp.dot(
            hidden[...], d_all[:, at], preferred_element_type=F32
        ).astype(BF)
        return carry

    lax.fori_loop(0, d_all.shape[1] // tile, outer, 0)


def expert_rows(rows, gate_pair, up_pair, down_pair):
    count, width = rows.shape
    hid = 2 * gate_pair[0].shape[2]
    whole = pl.BlockSpec(memory_space=pltpu.VMEM)
    there = pl.BlockSpec(memory_space=pltpu.HBM)
    return pl.pallas_call(
        expert_body,
        out_shape=jax.ShapeDtypeStruct((count, width), BF),
        in_specs=[whole] + [there] * 6,
        out_specs=whole,
        scratch_shapes=[
            pltpu.VMEM((width, hid), BF),
            pltpu.VMEM((width, hid), BF),
            pltpu.VMEM((hid, width), BF),
            pltpu.VMEM((count, hid), BF),
            pltpu.SemaphoreType.DMA((6,)),
        ],
        compiler_params=pltpu.CompilerParams(vmem_limit_bytes=28 * 1024 * 1024),
        cost_estimate=pl.CostEstimate(
            flops=6 * count * width * hid,
            bytes_accessed=6 * width * hid + 4 * count * width,
            transcendentals=count * hid,
        ),
    )(rows, *gate_pair, *up_pair, *down_pair)


def exchange(rows):
    width = rows.shape[1]
    out = lax.all_to_all(
        rows.reshape(PLANE, SLOTS, width), ("x", "y"), split_axis=0, concat_axis=0, tiled=True
    )
    return out.reshape(PLANE * SLOTS, width)


def local(
    queries,
    key_rows,
    value_rows,
    doc_lengths,
    residual_in,
    out_weight,
    norm_gain,
    expert_ids,
    gate_weights,
    w_gate,
    w_up,
    w_down,
):
    pairs = [(w, swap_cores(w)) for w in (w_gate, w_up, w_down)]
    attn_theirs, attn_mine = attend(queries, key_rows, value_rows, doc_lengths)
    mid = residual_in.astype(F32) + project(attn_theirs, attn_mine, out_weight)
    spread = jnp.mean(mid * mid, axis=1, keepdims=True)
    normed = (mid * lax.rsqrt(spread + 1e-06) * norm_gain[None, :]).astype(BF)

    rows, width = normed.shape
    meta = jnp.concatenate(
        [
            expert_ids.astype(BF),
            gate_weights.astype(BF),
            jnp.zeros((rows, META - 2 * TOP), BF),
        ],
        axis=1,
    )
    blocks, pairs = lax.optimization_barrier(
        (ring_gather(jnp.concatenate([normed, meta], axis=1), width // 2), pairs)
    )
    outgoing, weighted = dispatch(blocks, width)
    mine = exchange(outgoing)
    pair_out = expert_rows(mine, *pairs)
    returned = exchange(pair_out)
    plane_sum = lax.dot_general(
        weighted, returned, (((0,), (0,)), ((), ())), preferred_element_type=F32
    ).astype(BF)
    blocks = plane_sum.reshape(NZ, ROWS, -1)
    expert_sum = ring_sum({offset: blocks[i] for i, offset in enumerate(RING)})
    return (mid + expert_sum).astype(BF)


def solution(mesh):
    mesh = Mesh(mesh.devices.reshape(NX, NZ, NY, NC), ("x", "z", "y", "c"))
    seq, head = ("x", "z"), ("y", "c")
    every = seq + head
    placed = (
        P(seq, head),
        P(seq, None),
        P(seq, None),
        P(),
        P(every, None),
        P(head, None),
        P(),
        P(every, None),
        P(every, None),
        P(every, None, None),
        P(every, None, None),
        P(every, None, None),
    )
    return jax.shard_map(
        local, mesh=mesh, in_specs=placed, out_specs=P(every, None), check_vma=False
    )
```

```python
import functools
import math

import jax
import jax.numpy as jnp
from jax import lax
from jax.experimental import pallas as pl
from jax.experimental.pallas import tpu as pltpu
from jax.sharding import Mesh, PartitionSpec as P

HD = 128
NDOCS = 128
NX, NZ, NY, NC = 4, 8, 4, 2
ROWS = 64
CAP = 5
TOP = 8
META = 128
PLANE = NX * NY
SLOTS = NZ * CAP
NEAR = 5
NEAR_SLOTS = 24

BF = jnp.bfloat16
F32 = jnp.float32
masked_low = -1e30

RING = (0, -1, 1, -2, 2, -3, 3, 4)


def shift(value, axis, size, by):
    return lax.ppermute(value, axis, [(i, (i + by) % size) for i in range(size)])


def swap_cores(value):
    return lax.ppermute(value, "c", [(0, 1), (1, 0)])


def from_behind(value):
    devices = NX * NZ
    return lax.ppermute(value, ("x", "z"), [(i, i + 1) for i in range(devices - 1)])


def attend_half(base, queries, keys, values, lengths, store):
    rows = queries.shape[0]
    place = lax.broadcasted_iota(jnp.int32, (NDOCS, NDOCS), 0)
    upto = place <= lax.broadcasted_iota(jnp.int32, (NDOCS, NDOCS), 1)
    spread = jnp.broadcast_to(lengths.astype(F32), (8, NDOCS)).astype(BF)
    ends = jnp.dot(spread, jnp.where(upto, 1.0, 0.0).astype(BF), preferred_element_type=F32)[:1]
    query_pos = base + lax.broadcasted_iota(jnp.int32, (rows, 1), 0)
    ended = ends <= query_pos.astype(F32)
    start = jnp.max(jnp.where(ended, ends, 0.0), axis=1, keepdims=True).astype(jnp.int32)
    span = 2 * keys[0].shape[0]
    key_pos = base - keys[0].shape[0] + lax.broadcasted_iota(jnp.int32, (1, span), 1)
    visible = (key_pos <= query_pos) & (key_pos >= start)
    key_window = jnp.concatenate(keys, axis=0)
    value_window = jnp.concatenate(values, axis=0)
    for head in range(queries.shape[1] // HD):
        at = slice(head * HD, (head + 1) * HD)
        scores = lax.dot_general(
            queries[:, at], key_window, (((1,), (1,)), ((), ())), preferred_element_type=F32
        ) * (1.0 / math.sqrt(HD))
        scores = jnp.where(visible, scores, masked_low)
        weights = jnp.exp(scores - jnp.max(scores, axis=1, keepdims=True))
        total = jnp.sum(weights, axis=1, keepdims=True)
        mixture = jnp.dot(weights.astype(BF), value_window, preferred_element_type=F32)
        store(at, (mixture / total).astype(BF))


def late_body(where, q_ref, ka, kb, va, vb, len_ref, out_ref):
    def store(at, value):
        out_ref[:, at] = value

    attend_half(
        where[0] + q_ref.shape[0], q_ref[...], [ka[...], kb[...]], [va[...], vb[...]], len_ref[...], store
    )


def early_body(where, q_ref, tails, kb, vb, len_ref, late_ref, theirs_ref, mine_ref, held):
    rows = q_ref.shape[0]

    def store(at, value):
        held[:rows, at] = value

    held[rows:] = late_ref[...]
    attend_half(
        where[0], q_ref[...], [tails[0], kb[...]], [tails[1], vb[...]], len_ref[...], store
    )
    y, c = where[1], where[2]
    for k in range(NY):
        block = lax.rem(y + k, NY) * (NC * ROWS)
        here = pl.ds(pl.multiple_of(block + c * ROWS, ROWS), ROWS)
        there = pl.ds(pl.multiple_of(block + (1 - c) * ROWS, ROWS), ROWS)
        mine_ref[k * ROWS : (k + 1) * ROWS] = held[here]
        theirs_ref[k * ROWS : (k + 1) * ROWS] = held[there]


def attend(queries, key_rows, value_rows, doc_lengths):
    tok_rows, width = queries.shape
    half = tok_rows // 2
    y, c = lax.axis_index("y"), lax.axis_index("c")
    where = jnp.stack([lax.axis_index(("x", "z")) * tok_rows, y, c]).astype(jnp.int32)
    lengths = doc_lengths.reshape(1, -1)
    tails = from_behind(
        jnp.stack(
            [
                lax.dynamic_slice(rows, (half, y * HD), (half, HD))
                for rows in (key_rows, value_rows)
            ]
        )
    )

    def part(i):
        return pl.BlockSpec((half, HD), lambda g, where: (i, where[1]))

    def all_of(*shape):
        return pl.BlockSpec(shape, lambda g, where: (0,) * len(shape))

    lens = all_of(1, doc_lengths.shape[0])
    params = pltpu.CompilerParams(vmem_limit_bytes=57 * 1024 * 1024)
    scores = tok_rows * tok_rows * (width // HD) // 2
    late = pl.pallas_call(
        late_body,
        out_shape=jax.ShapeDtypeStruct((half, width), BF),
        grid_spec=pltpu.PrefetchScalarGridSpec(
            num_scalar_prefetch=1,
            grid=(1,),
            in_specs=[
                pl.BlockSpec((half, width), lambda g, where: (1, 0)),
                part(0),
                part(1),
                part(0),
                part(1),
                lens,
            ],
            out_specs=all_of(half, width),
        ),
        compiler_params=params,
        cost_estimate=pl.CostEstimate(
            flops=16 * scores * HD, bytes_accessed=6 * half * width, transcendentals=8 * scores
        ),
    )(where, queries, key_rows, key_rows, value_rows, value_rows, lengths)
    return pl.pallas_call(
        early_body,
        out_shape=(
            jax.ShapeDtypeStruct((half, width), BF),
            jax.ShapeDtypeStruct((half, width), BF),
        ),
        grid_spec=pltpu.PrefetchScalarGridSpec(
            num_scalar_prefetch=1,
            grid=(1,),
            in_specs=[
                pl.BlockSpec((half, width), lambda g, where: (0, 0)),
                all_of(2, half, HD),
                part(0),
                part(0),
                lens,
                all_of(half, width),
            ],
            out_specs=(all_of(half, width), all_of(half, width)),
            scratch_shapes=[pltpu.VMEM((tok_rows, width), BF)],
        ),
        compiler_params=params,
        cost_estimate=pl.CostEstimate(
            flops=16 * scores * HD, bytes_accessed=8 * half * width, transcendentals=8 * scores
        ),
    )(where, queries, tails, key_rows, value_rows, lengths, late)


def project(attn_theirs, attn_mine, out_weight):
    theirs = jnp.dot(attn_theirs, out_weight, preferred_element_type=F32).astype(BF)
    arrived = swap_cores(theirs)
    mine = lax.optimization_barrier(
        jnp.dot(attn_mine, out_weight, preferred_element_type=F32)
    )
    both = (mine + arrived.astype(F32)).reshape(NY, ROWS, out_weight.shape[1])
    sent = both.astype(BF)
    moved = [shift(sent[k], "y", NY, k) for k in range(1, NY)]
    return both[0] + sum(block.astype(F32) for block in moved)


def ring_gather(own, half):
    right = left = own
    blocks = [own]
    for _ in range(3):
        right = shift(right, "z", NZ, 1)
        left = shift(left, "z", NZ, -1)
        blocks += [right, left]
    return blocks + [shift(right[:, :half], "z", NZ, 1), shift(left[:, half:], "z", NZ, -1)]


def add(a, b):
    return (a.astype(F32) + b.astype(F32)).astype(BF)


def ring_sum_far(blocks):
    half = blocks[4].shape[1] // 2
    a = shift(blocks[4][:, :half], "z", NZ, 1)
    b = shift(blocks[4][:, half:], "z", NZ, -1)
    right = jnp.concatenate([add(blocks[3][:, :half], a), blocks[3][:, half:]], axis=1)
    left = jnp.concatenate([blocks[-3][:, :half], add(blocks[-3][:, half:], b)], axis=1)
    return shift(right, "z", NZ, 1), shift(left, "z", NZ, -1)


def ring_sum_near(right, left, blocks):
    for step in (2, 1):
        right = add(right, blocks[step])
        own = lax.optimization_barrier((blocks[-step], right))[0]
        left = add(left, own)
        right, left = shift(right, "z", NZ, 1), shift(left, "z", NZ, -1)
    return blocks[0].astype(F32) + right.astype(F32) + left.astype(F32)


def dispatch_body(first_block, first_slot, z_ref, *refs):
    blocks, (out_ref, weight_ref, tokens, meta, one_hot) = refs[:-5], refs[-5:]
    count, width = tokens.shape
    slots = out_ref.shape[0] // PLANE
    filled = 0
    column = 0
    for block in blocks:
        at = slice(filled, filled + ROWS)
        here = min(block.shape[1], width - column)
        tokens[at, column : column + here] = block[:, :here]
        column += here
        if block.shape[1] > here:
            meta[at] = block[:, here:]
        if column == width:
            filled, column = filled + ROWS, 0
    if filled < count:
        tokens[filled:] = jnp.zeros((count - filled, width), BF)
        meta[filled:] = jnp.full((count - filled, META), -1.0, BF)

    turned = meta[...].astype(F32).T
    ids, gates = turned[:TOP], turned[TOP : 2 * TOP]
    named, gate = [], []
    for place in range(PLANE):
        expert = (place // NY * NZ + z_ref[0]) * NY + place % NY
        match = ids == expert.astype(F32)
        named.append(jnp.max(jnp.where(match, 1.0, 0.0), axis=0, keepdims=True))
        gate.append(jnp.sum(jnp.where(match, gates, 0.0), axis=0, keepdims=True))
    first = lax.broadcasted_iota(jnp.int32, (count, count), 0)
    second = lax.broadcasted_iota(jnp.int32, (count, count), 1)
    before = (first < second) & (first // ROWS == second // ROWS)
    all_named = jnp.concatenate(named, axis=0)
    rank = jnp.dot(
        all_named.astype(BF), jnp.where(before, 1.0, 0.0).astype(BF), preferred_element_type=F32
    )
    start = (lax.broadcasted_iota(jnp.int32, (1, count), 1) // ROWS + first_block) * CAP
    slot = jnp.where(all_named > 0.0, rank + start.astype(F32), -1.0)
    numbers = (first_slot + lax.broadcasted_iota(jnp.int32, (slots, 1), 0)).astype(F32)
    for pair in range(PLANE // 2):
        hits, weights = [], []
        for place in (2 * pair, 2 * pair + 1):
            hit = slot[place : place + 1] == numbers
            hits.append(jnp.where(hit, 1.0, 0.0))
            weights.append(jnp.where(hit, gate[place], 0.0))
        at = slice(2 * pair * slots, (2 * pair + 2) * slots)
        one_hot[at] = jnp.concatenate(hits, axis=0).astype(BF)
        weight_ref[at] = jnp.concatenate(weights, axis=0).astype(BF)
    tile = 256

    def fill(i, carry):
        at = pl.ds(pl.multiple_of(i * tile, tile), tile)
        out_ref[:, at] = jnp.dot(
            one_hot[...], tokens[:, at], preferred_element_type=F32
        ).astype(BF)
        return carry

    lax.fori_loop(0, width // tile, fill, 0)


def dispatch(blocks, first_block, first_slot, slots, width):
    filled = ROWS * (sum(block.shape[1] for block in blocks) // width)
    count = -(-filled // 128) * 128
    whole = pl.BlockSpec(memory_space=pltpu.VMEM)
    return pl.pallas_call(
        functools.partial(dispatch_body, first_block, first_slot),
        out_shape=(
            jax.ShapeDtypeStruct((PLANE * slots, width), BF),
            jax.ShapeDtypeStruct((PLANE * slots, count), BF),
        ),
        in_specs=[pl.BlockSpec(memory_space=pltpu.SMEM)] + [whole] * len(blocks),
        out_specs=(whole, whole),
        scratch_shapes=[
            pltpu.VMEM((count, width), BF),
            pltpu.VMEM((count, META), BF),
            pltpu.VMEM((PLANE * slots, count), BF),
        ],
        compiler_params=pltpu.CompilerParams(vmem_limit_bytes=24 * 1024 * 1024),
        cost_estimate=pl.CostEstimate(
            flops=2 * PLANE * slots * count * width,
            bytes_accessed=4 * count * width,
            transcendentals=0,
        ),
    )(lax.axis_index("z").astype(jnp.int32).reshape(1), *blocks)


def expert_body(rows_ref, g0, g1, u0, u1, d0, d1, out_ref, g_all, u_all, d_all, hidden, sems):
    half = g0.shape[2]
    copies = [
        pltpu.make_async_copy(g0.at[0], g_all.at[:, :half], sems.at[0]),
        pltpu.make_async_copy(g1.at[0], g_all.at[:, half:], sems.at[1]),
        pltpu.make_async_copy(u0.at[0], u_all.at[:, :half], sems.at[2]),
        pltpu.make_async_copy(u1.at[0], u_all.at[:, half:], sems.at[3]),
        pltpu.make_async_copy(d0.at[0], d_all.at[:half], sems.at[4]),
        pltpu.make_async_copy(d1.at[0], d_all.at[half:], sems.at[5]),
    ]
    for which in (0, 2, 1, 3, 4, 5):
        copies[which].start()
    tile = 256
    for i in range(g_all.shape[1] // tile):
        if i == 0:
            copies[0].wait()
            copies[2].wait()
        if i == half // tile:
            copies[1].wait()
            copies[3].wait()
        at = slice(i * tile, (i + 1) * tile)
        gate_act = jnp.dot(rows_ref[...], g_all[:, at], preferred_element_type=F32)
        up_act = jnp.dot(rows_ref[...], u_all[:, at], preferred_element_type=F32)
        hidden[:, at] = (gate_act / (1.0 + jnp.exp(-gate_act)) * up_act).astype(BF)
    for copy in copies[4:]:
        copy.wait()

    def outer(i, carry):
        at = pl.ds(pl.multiple_of(i * tile, tile), tile)
        out_ref[:, at] = jnp.dot(
            hidden[...], d_all[:, at], preferred_element_type=F32
        ).astype(BF)
        return carry

    lax.fori_loop(0, d_all.shape[1] // tile, outer, 0)


def expert_rows(rows, gate_pair, up_pair, down_pair):
    count, width = rows.shape
    hid = 2 * gate_pair[0].shape[2]
    whole = pl.BlockSpec(memory_space=pltpu.VMEM)
    there = pl.BlockSpec(memory_space=pltpu.HBM)
    return pl.pallas_call(
        expert_body,
        out_shape=jax.ShapeDtypeStruct((count, width), BF),
        in_specs=[whole] + [there] * 6,
        out_specs=whole,
        scratch_shapes=[
            pltpu.VMEM((width, hid), BF),
            pltpu.VMEM((width, hid), BF),
            pltpu.VMEM((hid, width), BF),
            pltpu.VMEM((count, hid), BF),
            pltpu.SemaphoreType.DMA((6,)),
        ],
        compiler_params=pltpu.CompilerParams(vmem_limit_bytes=57 * 1024 * 1024),
        cost_estimate=pl.CostEstimate(
            flops=6 * count * width * hid,
            bytes_accessed=6 * width * hid + 4 * count * width,
            transcendentals=count * hid,
        ),
    )(rows, *gate_pair, *up_pair, *down_pair)


def exchange(rows):
    count, width = rows.shape
    out = lax.all_to_all(
        rows.reshape(PLANE, count // PLANE, width),
        ("x", "y"),
        split_axis=0,
        concat_axis=0,
        tiled=True,
    )
    return out.reshape(count, width)


def weighted_sum(weights, rows):
    return lax.dot_general(weights, rows, (((0,), (0,)), ((), ())), preferred_element_type=F32)


def local(
    queries,
    key_rows,
    value_rows,
    doc_lengths,
    residual_in,
    out_weight,
    norm_gain,
    expert_ids,
    gate_weights,
    w_gate,
    w_up,
    w_down,
):
    pairs = [(w, swap_cores(w)) for w in (w_gate, w_up, w_down)]
    attn_theirs, attn_mine = attend(queries, key_rows, value_rows, doc_lengths)
    mid = residual_in.astype(F32) + project(attn_theirs, attn_mine, out_weight)
    spread = jnp.mean(mid * mid, axis=1, keepdims=True)
    normed = (mid * lax.rsqrt(spread + 1e-06) * norm_gain[None, :]).astype(BF)

    rows, width = normed.shape
    meta = jnp.concatenate(
        [
            expert_ids.astype(BF),
            gate_weights.astype(BF),
            jnp.zeros((rows, META - 2 * TOP), BF),
        ],
        axis=1,
    )
    blocks = ring_gather(jnp.concatenate([normed, meta], axis=1), width // 2)
    out_near, weight_near = dispatch(blocks[:NEAR], 0, 0, NEAR_SLOTS, width)
    arrived_near = exchange(out_near)
    far_blocks, pairs = lax.optimization_barrier((blocks[NEAR - 1 :], pairs))
    out_far, weight_far = dispatch(
        far_blocks, NEAR - 1, NEAR_SLOTS, SLOTS - NEAR_SLOTS, width
    )
    out_far, arrived_near = lax.optimization_barrier((out_far, arrived_near))
    arrived_far = exchange(out_far)
    pair_near = expert_rows(arrived_near, *pairs)
    arrived_far, pair_near = lax.optimization_barrier((arrived_far, pair_near))
    pair_far = expert_rows(arrived_far, *pairs)

    returned_far = exchange(pair_far)
    returned_far, pair_near = lax.optimization_barrier((returned_far, pair_near))
    returned_near = exchange(pair_near)
    far = weighted_sum(weight_far, returned_far).reshape(-1, ROWS, width)
    terms = {offset: far[1 + i].astype(BF) for i, offset in enumerate(RING[NEAR:])}
    right, left = ring_sum_far(terms)
    near = weighted_sum(weight_near, returned_near)[: NEAR * ROWS].reshape(NEAR, ROWS, width)
    terms = {offset: near[i].astype(BF) for i, offset in enumerate(RING[: NEAR - 1])}
    terms[RING[NEAR - 1]] = (near[NEAR - 1] + far[0]).astype(BF)
    expert_sum = ring_sum_near(right, left, terms)
    return (mid + expert_sum).astype(BF)


def solution(mesh):
    mesh = Mesh(mesh.devices.reshape(NX, NZ, NY, NC), ("x", "z", "y", "c"))
    seq, head = ("x", "z"), ("y", "c")
    every = seq + head
    placed = (
        P(seq, head),
        P(seq, None),
        P(seq, None),
        P(),
        P(every, None),
        P(head, None),
        P(),
        P(every, None),
        P(every, None),
        P(every, None, None),
        P(every, None, None),
        P(every, None, None),
    )
    return jax.shard_map(
        local, mesh=mesh, in_specs=placed, out_specs=P(every, None), check_vma=False
    )
```

```python
import functools
import math

import jax
import jax.numpy as jnp
from jax import lax
from jax.experimental import pallas as pl
from jax.experimental.pallas import tpu as pltpu
from jax.sharding import Mesh, PartitionSpec as P

HD = 128
NDOCS = 128
NX, NZ, NY, NC = 4, 8, 4, 2
ROWS = 64
CAP = 5
TOP = 8
META = 128
PLANE = NX * NY
SLOTS = NZ * CAP
NEAR = 5
NEAR_SLOTS = 24

BF = jnp.bfloat16
F32 = jnp.float32
masked_low = -1e30

RING = (0, -1, -2, 2, 1, -3, 3, 4)


def shift(value, axis, size, by):
    return lax.ppermute(value, axis, [(i, (i + by) % size) for i in range(size)])


def swap_cores(value):
    return lax.ppermute(value, "c", [(0, 1), (1, 0)])


def from_behind(value):
    devices = NX * NZ
    return lax.ppermute(value, ("x", "z"), [(i, i + 1) for i in range(devices - 1)])


def attend_half(base, queries, keys, values, lengths, store):
    rows = queries.shape[0]
    place = lax.broadcasted_iota(jnp.int32, (NDOCS, NDOCS), 0)
    upto = place <= lax.broadcasted_iota(jnp.int32, (NDOCS, NDOCS), 1)
    spread = jnp.broadcast_to(lengths.astype(F32), (8, NDOCS)).astype(BF)
    ends = jnp.dot(spread, jnp.where(upto, 1.0, 0.0).astype(BF), preferred_element_type=F32)[:1]
    query_pos = base + lax.broadcasted_iota(jnp.int32, (rows, 1), 0)
    ended = ends <= query_pos.astype(F32)
    start = jnp.max(jnp.where(ended, ends, 0.0), axis=1, keepdims=True).astype(jnp.int32)
    span = 2 * keys[0].shape[0]
    key_pos = base - keys[0].shape[0] + lax.broadcasted_iota(jnp.int32, (1, span), 1)
    visible = (key_pos <= query_pos) & (key_pos >= start)
    key_window = jnp.concatenate(keys, axis=0)
    value_window = jnp.concatenate(values, axis=0)
    for head in range(queries.shape[1] // HD):
        at = slice(head * HD, (head + 1) * HD)
        scores = lax.dot_general(
            queries[:, at], key_window, (((1,), (1,)), ((), ())), preferred_element_type=F32
        ) * (1.0 / math.sqrt(HD))
        scores = jnp.where(visible, scores, masked_low)
        weights = jnp.exp(scores - jnp.max(scores, axis=1, keepdims=True))
        total = jnp.sum(weights, axis=1, keepdims=True)
        mixture = jnp.dot(weights.astype(BF), value_window, preferred_element_type=F32)
        store(at, (mixture / total).astype(BF))


def late_body(where, q_ref, ka, kb, va, vb, len_ref, out_ref):
    def store(at, value):
        out_ref[:, at] = value

    attend_half(
        where[0] + q_ref.shape[0], q_ref[...], [ka[...], kb[...]], [va[...], vb[...]], len_ref[...], store
    )


def early_body(where, q_ref, tails, kb, vb, len_ref, late_ref, theirs_ref, mine_ref, held):
    rows = q_ref.shape[0]

    def store(at, value):
        held[:rows, at] = value

    held[rows:] = late_ref[...]
    attend_half(
        where[0], q_ref[...], [tails[0], kb[...]], [tails[1], vb[...]], len_ref[...], store
    )
    y, c = where[1], where[2]
    for k in range(NY):
        block = lax.rem(y + k, NY) * (NC * ROWS)
        here = pl.ds(pl.multiple_of(block + c * ROWS, ROWS), ROWS)
        there = pl.ds(pl.multiple_of(block + (1 - c) * ROWS, ROWS), ROWS)
        mine_ref[k * ROWS : (k + 1) * ROWS] = held[here]
        theirs_ref[k * ROWS : (k + 1) * ROWS] = held[there]


def attend(queries, key_rows, value_rows, doc_lengths):
    tok_rows, width = queries.shape
    half = tok_rows // 2
    y, c = lax.axis_index("y"), lax.axis_index("c")
    where = jnp.stack([lax.axis_index(("x", "z")) * tok_rows, y, c]).astype(jnp.int32)
    lengths = doc_lengths.reshape(1, -1)
    tails = from_behind(
        jnp.stack(
            [
                lax.dynamic_slice(rows, (half, y * HD), (half, HD))
                for rows in (key_rows, value_rows)
            ]
        )
    )

    def part(i):
        return pl.BlockSpec((half, HD), lambda g, where: (i, where[1]))

    def all_of(*shape):
        return pl.BlockSpec(shape, lambda g, where: (0,) * len(shape))

    lens = all_of(1, doc_lengths.shape[0])
    params = pltpu.CompilerParams(vmem_limit_bytes=57 * 1024 * 1024)
    scores = tok_rows * tok_rows * (width // HD) // 2
    late = pl.pallas_call(
        late_body,
        out_shape=jax.ShapeDtypeStruct((half, width), BF),
        grid_spec=pltpu.PrefetchScalarGridSpec(
            num_scalar_prefetch=1,
            grid=(1,),
            in_specs=[
                pl.BlockSpec((half, width), lambda g, where: (1, 0)),
                part(0),
                part(1),
                part(0),
                part(1),
                lens,
            ],
            out_specs=all_of(half, width),
        ),
        compiler_params=params,
        cost_estimate=pl.CostEstimate(
            flops=16 * scores * HD, bytes_accessed=6 * half * width, transcendentals=8 * scores
        ),
    )(where, queries, key_rows, key_rows, value_rows, value_rows, lengths)
    return pl.pallas_call(
        early_body,
        out_shape=(
            jax.ShapeDtypeStruct((half, width), BF),
            jax.ShapeDtypeStruct((half, width), BF),
        ),
        grid_spec=pltpu.PrefetchScalarGridSpec(
            num_scalar_prefetch=1,
            grid=(1,),
            in_specs=[
                pl.BlockSpec((half, width), lambda g, where: (0, 0)),
                all_of(2, half, HD),
                part(0),
                part(0),
                lens,
                all_of(half, width),
            ],
            out_specs=(all_of(half, width), all_of(half, width)),
            scratch_shapes=[pltpu.VMEM((tok_rows, width), BF)],
        ),
        compiler_params=params,
        cost_estimate=pl.CostEstimate(
            flops=16 * scores * HD, bytes_accessed=8 * half * width, transcendentals=8 * scores
        ),
    )(where, queries, tails, key_rows, value_rows, lengths, late)


def project(attn_theirs, attn_mine, out_weight, other_weight):
    arrived = swap_cores(attn_theirs)
    mine = lax.optimization_barrier(
        jnp.dot(attn_mine, out_weight, preferred_element_type=F32)
    )
    both = mine + jnp.dot(arrived, other_weight, preferred_element_type=F32)
    both = both.reshape(NY, ROWS, out_weight.shape[1])
    sent = both.astype(BF)
    moved = [shift(sent[k], "y", NY, k) for k in range(1, NY)]
    return both[0] + sum(block.astype(F32) for block in moved)


def ring_gather(own, half):
    blocks = {0: own}
    right = left = own
    for hops in (1, 2, 3):
        right = blocks[-hops] = shift(right, "z", NZ, 1)
        left = blocks[hops] = shift(left, "z", NZ, -1)
    last = [shift(right[:, :half], "z", NZ, 1), shift(left[:, half:], "z", NZ, -1)]
    return [blocks[offset] for offset in RING[:-1]] + last


def add(a, b):
    return (a.astype(F32) + b.astype(F32)).astype(BF)


def ring_sum_far(blocks):
    half = blocks[4].shape[1] // 2
    a = shift(blocks[4][:, :half], "z", NZ, 1)
    b = shift(blocks[4][:, half:], "z", NZ, -1)
    right = jnp.concatenate([add(blocks[3][:, :half], a), blocks[3][:, half:]], axis=1)
    left = jnp.concatenate([blocks[-3][:, :half], add(blocks[-3][:, half:], b)], axis=1)
    return shift(right, "z", NZ, 1), shift(left, "z", NZ, -1)


def ring_step(right, left, to_right, to_left):
    right = add(right, to_right)
    to_left = lax.optimization_barrier((to_left, right))[0]
    left = add(left, to_left)
    return right, left


def dispatch_body(first_block, first_slot, z_ref, *refs):
    blocks, (out_ref, weight_ref, tokens, meta, one_hot) = refs[:-5], refs[-5:]
    count, width = tokens.shape
    slots = out_ref.shape[0] // PLANE
    filled = 0
    column = 0
    for block in blocks:
        at = slice(filled, filled + ROWS)
        here = min(block.shape[1], width - column)
        tokens[at, column : column + here] = block[:, :here]
        column += here
        if block.shape[1] > here:
            meta[at] = block[:, here:]
        if column == width:
            filled, column = filled + ROWS, 0
    if filled < count:
        tokens[filled:] = jnp.zeros((count - filled, width), BF)
        meta[filled:] = jnp.full((count - filled, META), -1.0, BF)

    turned = meta[...].astype(F32).T
    ids, gates = turned[:TOP], turned[TOP : 2 * TOP]
    named, gate = [], []
    for place in range(PLANE):
        expert = (place // NY * NZ + z_ref[0]) * NY + place % NY
        match = ids == expert.astype(F32)
        named.append(jnp.max(jnp.where(match, 1.0, 0.0), axis=0, keepdims=True))
        gate.append(jnp.sum(jnp.where(match, gates, 0.0), axis=0, keepdims=True))
    first = lax.broadcasted_iota(jnp.int32, (count, count), 0)
    second = lax.broadcasted_iota(jnp.int32, (count, count), 1)
    before = (first < second) & (first // ROWS == second // ROWS)
    all_named = jnp.concatenate(named, axis=0)
    rank = jnp.dot(
        all_named.astype(BF), jnp.where(before, 1.0, 0.0).astype(BF), preferred_element_type=F32
    )
    start = (lax.broadcasted_iota(jnp.int32, (1, count), 1) // ROWS + first_block) * CAP
    slot = jnp.where(all_named > 0.0, rank + start.astype(F32), -1.0)
    numbers = (first_slot + lax.broadcasted_iota(jnp.int32, (slots, 1), 0)).astype(F32)
    for pair in range(PLANE // 2):
        hits, weights = [], []
        for place in (2 * pair, 2 * pair + 1):
            hit = slot[place : place + 1] == numbers
            hits.append(jnp.where(hit, 1.0, 0.0))
            weights.append(jnp.where(hit, gate[place], 0.0))
        at = slice(2 * pair * slots, (2 * pair + 2) * slots)
        one_hot[at] = jnp.concatenate(hits, axis=0).astype(BF)
        weight_ref[at] = jnp.concatenate(weights, axis=0).astype(BF)
    tile = 256

    def fill(i, carry):
        at = pl.ds(pl.multiple_of(i * tile, tile), tile)
        out_ref[:, at] = jnp.dot(
            one_hot[...], tokens[:, at], preferred_element_type=F32
        ).astype(BF)
        return carry

    lax.fori_loop(0, width // tile, fill, 0)


def dispatch(blocks, first_block, first_slot, slots, width):
    filled = ROWS * (sum(block.shape[1] for block in blocks) // width)
    count = -(-filled // 128) * 128
    whole = pl.BlockSpec(memory_space=pltpu.VMEM)
    return pl.pallas_call(
        functools.partial(dispatch_body, first_block, first_slot),
        out_shape=(
            jax.ShapeDtypeStruct((PLANE * slots, width), BF),
            jax.ShapeDtypeStruct((PLANE * slots, count), BF),
        ),
        in_specs=[pl.BlockSpec(memory_space=pltpu.SMEM)] + [whole] * len(blocks),
        out_specs=(whole, whole),
        scratch_shapes=[
            pltpu.VMEM((count, width), BF),
            pltpu.VMEM((count, META), BF),
            pltpu.VMEM((PLANE * slots, count), BF),
        ],
        compiler_params=pltpu.CompilerParams(vmem_limit_bytes=24 * 1024 * 1024),
        cost_estimate=pl.CostEstimate(
            flops=2 * PLANE * slots * count * width,
            bytes_accessed=4 * count * width,
            transcendentals=0,
        ),
    )(lax.axis_index("z").astype(jnp.int32).reshape(1), *blocks)


def expert_body(rows_ref, g0, g1, u0, u1, d0, d1, out_ref, g_all, u_all, d_all, hidden, sems):
    half = g0.shape[2]
    copies = [
        pltpu.make_async_copy(g0.at[0], g_all.at[:, :half], sems.at[0]),
        pltpu.make_async_copy(g1.at[0], g_all.at[:, half:], sems.at[1]),
        pltpu.make_async_copy(u0.at[0], u_all.at[:, :half], sems.at[2]),
        pltpu.make_async_copy(u1.at[0], u_all.at[:, half:], sems.at[3]),
        pltpu.make_async_copy(d0.at[0], d_all.at[:half], sems.at[4]),
        pltpu.make_async_copy(d1.at[0], d_all.at[half:], sems.at[5]),
    ]
    for which in (0, 2, 1, 3, 4, 5):
        copies[which].start()
    tile = 256
    for i in range(g_all.shape[1] // tile):
        if i == 0:
            copies[0].wait()
            copies[2].wait()
        if i == half // tile:
            copies[1].wait()
            copies[3].wait()
        at = slice(i * tile, (i + 1) * tile)
        gate_act = jnp.dot(rows_ref[...], g_all[:, at], preferred_element_type=F32)
        up_act = jnp.dot(rows_ref[...], u_all[:, at], preferred_element_type=F32)
        hidden[:, at] = (gate_act / (1.0 + jnp.exp(-gate_act)) * up_act).astype(BF)
    for copy in copies[4:]:
        copy.wait()

    def outer(i, carry):
        at = pl.ds(pl.multiple_of(i * tile, tile), tile)
        out_ref[:, at] = jnp.dot(
            hidden[...], d_all[:, at], preferred_element_type=F32
        ).astype(BF)
        return carry

    lax.fori_loop(0, d_all.shape[1] // tile, outer, 0)


def expert_rows(rows, gate_pair, up_pair, down_pair):
    count, width = rows.shape
    hid = 2 * gate_pair[0].shape[2]
    whole = pl.BlockSpec(memory_space=pltpu.VMEM)
    there = pl.BlockSpec(memory_space=pltpu.HBM)
    return pl.pallas_call(
        expert_body,
        out_shape=jax.ShapeDtypeStruct((count, width), BF),
        in_specs=[whole] + [there] * 6,
        out_specs=whole,
        scratch_shapes=[
            pltpu.VMEM((width, hid), BF),
            pltpu.VMEM((width, hid), BF),
            pltpu.VMEM((hid, width), BF),
            pltpu.VMEM((count, hid), BF),
            pltpu.SemaphoreType.DMA((6,)),
        ],
        compiler_params=pltpu.CompilerParams(vmem_limit_bytes=57 * 1024 * 1024),
        cost_estimate=pl.CostEstimate(
            flops=6 * count * width * hid,
            bytes_accessed=6 * width * hid + 4 * count * width,
            transcendentals=count * hid,
        ),
    )(rows, *gate_pair, *up_pair, *down_pair)


def exchange(rows):
    count, width = rows.shape
    out = lax.all_to_all(
        rows.reshape(PLANE, count // PLANE, width),
        ("x", "y"),
        split_axis=0,
        concat_axis=0,
        tiled=True,
    )
    return out.reshape(count, width)


def weighted_sum(weights, rows):
    return lax.dot_general(weights, rows, (((0,), (0,)), ((), ())), preferred_element_type=F32)


def local(
    queries,
    key_rows,
    value_rows,
    doc_lengths,
    residual_in,
    out_weight,
    norm_gain,
    expert_ids,
    gate_weights,
    w_gate,
    w_up,
    w_down,
):
    pairs = [(w, swap_cores(w)) for w in (w_gate, w_up, w_down)]
    other_weight = swap_cores(out_weight)
    attn_theirs, attn_mine = attend(queries, key_rows, value_rows, doc_lengths)
    mid = residual_in.astype(F32) + project(attn_theirs, attn_mine, out_weight, other_weight)
    spread = jnp.mean(mid * mid, axis=1, keepdims=True)
    normed = (mid * lax.rsqrt(spread + 1e-06) * norm_gain[None, :]).astype(BF)

    normed, pairs = lax.optimization_barrier((normed, pairs))
    rows, width = normed.shape
    meta = jnp.concatenate(
        [
            expert_ids.astype(BF),
            gate_weights.astype(BF),
            jnp.zeros((rows, META - 2 * TOP), BF),
        ],
        axis=1,
    )
    blocks = ring_gather(jnp.concatenate([normed, meta], axis=1), width // 2)
    out_near, weight_near = dispatch(blocks[:NEAR], 0, 0, NEAR_SLOTS, width)
    arrived_near = exchange(out_near)
    out_far, weight_far = dispatch(
        blocks[NEAR - 1 :], NEAR - 1, NEAR_SLOTS, SLOTS - NEAR_SLOTS, width
    )
    out_far, arrived_near = lax.optimization_barrier((out_far, arrived_near))
    arrived_far = exchange(out_far)
    pair_near = expert_rows(arrived_near, *pairs)
    arrived_far, pair_near = lax.optimization_barrier((arrived_far, pair_near))
    pair_far = expert_rows(arrived_far, *pairs)

    returned_far = exchange(pair_far)
    returned_far, pair_near = lax.optimization_barrier((returned_far, pair_near))
    returned_near = exchange(pair_near)
    far = weighted_sum(weight_far, returned_far).reshape(-1, ROWS, width)
    terms = {offset: far[1 + i].astype(BF) for i, offset in enumerate(RING[NEAR:])}
    right, left = ring_sum_far(terms)

    def near_terms(first, rows):
        picked = weight_near[:, first * ROWS : (first + 2) * ROWS]
        return weighted_sum(picked, rows).reshape(2, ROWS, width)

    to_left, to_right = near_terms(2, returned_near).astype(BF)
    right, left = ring_step(right, left, to_right, to_left)
    returned_near = lax.optimization_barrier((returned_near, right, left))[0]
    right, left = shift(right, "z", NZ, 1), shift(left, "z", NZ, -1)
    own, to_left = near_terms(0, returned_near)
    to_right = near_terms(4, returned_near)[0] + far[0]
    right, left = ring_step(right, left, to_right.astype(BF), to_left.astype(BF))
    right, left = shift(right, "z", NZ, 1), shift(left, "z", NZ, -1)
    expert_sum = own + right.astype(F32) + left.astype(F32)
    return (mid + expert_sum).astype(BF)


def solution(mesh):
    mesh = Mesh(mesh.devices.reshape(NX, NZ, NY, NC), ("x", "z", "y", "c"))
    seq, head = ("x", "z"), ("y", "c")
    every = seq + head
    placed = (
        P(seq, head),
        P(seq, None),
        P(seq, None),
        P(),
        P(every, None),
        P(head, None),
        P(),
        P(every, None),
        P(every, None),
        P(every, None, None),
        P(every, None, None),
        P(every, None, None),
    )
    return jax.shard_map(
        local, mesh=mesh, in_specs=placed, out_specs=P(every, None), check_vma=False
    )
```

```python
import functools
import math

import jax
import jax.numpy as jnp
from jax import lax
from jax.experimental import pallas as pl
from jax.experimental.pallas import tpu as pltpu
from jax.sharding import Mesh, PartitionSpec as P

HD = 128
NDOCS = 128
NX, NZ, NY, NC = 4, 8, 4, 2
ROWS = 64
CAP = 5
TOP = 8
META = 128
PLANE = NX * NY
SLOTS = NZ * CAP
NEAR = 5
NEAR_SLOTS = 24

BF = jnp.bfloat16
F32 = jnp.float32
masked_low = -1e30

RING = (0, -1, -2, 2, 1, -3, 3, 4)


def shift(value, axis, size, by):
    return lax.ppermute(value, axis, [(i, (i + by) % size) for i in range(size)])


def swap_cores(value):
    return lax.ppermute(value, "c", [(0, 1), (1, 0)])


def from_behind(value):
    devices = NX * NZ
    return lax.ppermute(value, ("x", "z"), [(i, i + 1) for i in range(devices - 1)])


def attend_half(base, queries, keys, values, lengths, store):
    rows = queries.shape[0]
    place = lax.broadcasted_iota(jnp.int32, (NDOCS, NDOCS), 0)
    upto = place <= lax.broadcasted_iota(jnp.int32, (NDOCS, NDOCS), 1)
    spread = jnp.broadcast_to(lengths.astype(F32), (8, NDOCS)).astype(BF)
    ends = jnp.dot(spread, jnp.where(upto, 1.0, 0.0).astype(BF), preferred_element_type=F32)[:1]
    query_pos = base + lax.broadcasted_iota(jnp.int32, (rows, 1), 0)
    ended = ends <= query_pos.astype(F32)
    start = jnp.max(jnp.where(ended, ends, 0.0), axis=1, keepdims=True).astype(jnp.int32)
    span = 2 * keys[0].shape[0]
    key_pos = base - keys[0].shape[0] + lax.broadcasted_iota(jnp.int32, (1, span), 1)
    visible = (key_pos <= query_pos) & (key_pos >= start)
    key_window = jnp.concatenate(keys, axis=0)
    value_window = jnp.concatenate(values, axis=0)
    for head in range(queries.shape[1] // HD):
        at = slice(head * HD, (head + 1) * HD)
        scores = lax.dot_general(
            queries[:, at], key_window, (((1,), (1,)), ((), ())), preferred_element_type=F32
        ) * (1.0 / math.sqrt(HD))
        scores = jnp.where(visible, scores, masked_low)
        weights = jnp.exp(scores - jnp.max(scores, axis=1, keepdims=True))
        total = jnp.sum(weights, axis=1, keepdims=True)
        mixture = jnp.dot(weights.astype(BF), value_window, preferred_element_type=F32)
        store(at, (mixture / total).astype(BF))


def late_body(where, q_ref, ka, kb, va, vb, len_ref, out_ref):
    def store(at, value):
        out_ref[:, at] = value

    attend_half(
        where[0] + q_ref.shape[0], q_ref[...], [ka[...], kb[...]], [va[...], vb[...]], len_ref[...], store
    )


def early_body(where, q_ref, tails, kb, vb, len_ref, late_ref, theirs_ref, mine_ref, held):
    rows = q_ref.shape[0]

    def store(at, value):
        held[:rows, at] = value

    held[rows:] = late_ref[...]
    attend_half(
        where[0], q_ref[...], [tails[0], kb[...]], [tails[1], vb[...]], len_ref[...], store
    )
    y, c = where[1], where[2]
    for k in range(NY):
        block = lax.rem(y + k, NY) * (NC * ROWS)
        here = pl.ds(pl.multiple_of(block + c * ROWS, ROWS), ROWS)
        there = pl.ds(pl.multiple_of(block + (1 - c) * ROWS, ROWS), ROWS)
        mine_ref[k * ROWS : (k + 1) * ROWS] = held[here]
        theirs_ref[k * ROWS : (k + 1) * ROWS] = held[there]


def attend(queries, key_rows, value_rows, doc_lengths):
    tok_rows, width = queries.shape
    half = tok_rows // 2
    y, c = lax.axis_index("y"), lax.axis_index("c")
    where = jnp.stack([lax.axis_index(("x", "z")) * tok_rows, y, c]).astype(jnp.int32)
    lengths = doc_lengths.reshape(1, -1)
    tails = from_behind(
        jnp.stack(
            [
                lax.dynamic_slice(rows, (half, y * HD), (half, HD))
                for rows in (key_rows, value_rows)
            ]
        )
    )

    def part(i):
        return pl.BlockSpec((half, HD), lambda g, where: (i, where[1]))

    def all_of(*shape):
        return pl.BlockSpec(shape, lambda g, where: (0,) * len(shape))

    lens = all_of(1, doc_lengths.shape[0])
    params = pltpu.CompilerParams(vmem_limit_bytes=57 * 1024 * 1024)
    scores = tok_rows * tok_rows * (width // HD) // 2
    late = pl.pallas_call(
        late_body,
        out_shape=jax.ShapeDtypeStruct((half, width), BF),
        grid_spec=pltpu.PrefetchScalarGridSpec(
            num_scalar_prefetch=1,
            grid=(1,),
            in_specs=[
                pl.BlockSpec((half, width), lambda g, where: (1, 0)),
                part(0),
                part(1),
                part(0),
                part(1),
                lens,
            ],
            out_specs=all_of(half, width),
        ),
        compiler_params=params,
        cost_estimate=pl.CostEstimate(
            flops=16 * scores * HD, bytes_accessed=6 * half * width, transcendentals=8 * scores
        ),
    )(where, queries, key_rows, key_rows, value_rows, value_rows, lengths)
    return pl.pallas_call(
        early_body,
        out_shape=(
            jax.ShapeDtypeStruct((half, width), BF),
            jax.ShapeDtypeStruct((half, width), BF),
        ),
        grid_spec=pltpu.PrefetchScalarGridSpec(
            num_scalar_prefetch=1,
            grid=(1,),
            in_specs=[
                pl.BlockSpec((half, width), lambda g, where: (0, 0)),
                all_of(2, half, HD),
                part(0),
                part(0),
                lens,
                all_of(half, width),
            ],
            out_specs=(all_of(half, width), all_of(half, width)),
            scratch_shapes=[pltpu.VMEM((tok_rows, width), BF)],
        ),
        compiler_params=params,
        cost_estimate=pl.CostEstimate(
            flops=16 * scores * HD, bytes_accessed=8 * half * width, transcendentals=8 * scores
        ),
    )(where, queries, tails, key_rows, value_rows, lengths, late)


def project(attn_theirs, attn_mine, out_weight, other_weight):
    arrived = swap_cores(attn_theirs)
    mine = lax.optimization_barrier(
        jnp.dot(attn_mine, out_weight, preferred_element_type=F32)
    )
    both = mine + jnp.dot(arrived, other_weight, preferred_element_type=F32)
    both = both.reshape(NY, ROWS, out_weight.shape[1])
    sent = both.astype(BF)
    moved = [shift(sent[k], "y", NY, k) for k in range(1, NY)]
    return both[0] + sum(block.astype(F32) for block in moved)


def ring_gather(own, half):
    blocks = {0: own}
    right = left = own
    for hops in (1, 2, 3):
        right = blocks[-hops] = shift(right, "z", NZ, 1)
        left = blocks[hops] = shift(left, "z", NZ, -1)
    last = [shift(right[:, :half], "z", NZ, 1), shift(left[:, half:], "z", NZ, -1)]
    return [blocks[offset] for offset in RING[:-1]] + last


def add(a, b):
    return (a.astype(F32) + b.astype(F32)).astype(BF)


def ring_step(right, left, to_right, to_left):
    right = add(right, to_right)
    to_left = lax.optimization_barrier((to_left, right))[0]
    left = add(left, to_left)
    return right, left


def dispatch_body(first_block, first_slot, z_ref, *refs):
    blocks, (out_ref, weight_ref, tokens, meta, one_hot) = refs[:-5], refs[-5:]
    count, width = tokens.shape
    slots = out_ref.shape[0] // PLANE
    filled = 0
    column = 0
    for block in blocks:
        at = slice(filled, filled + ROWS)
        here = min(block.shape[1], width - column)
        tokens[at, column : column + here] = block[:, :here]
        column += here
        if block.shape[1] > here:
            meta[at] = block[:, here:]
        if column == width:
            filled, column = filled + ROWS, 0
    if filled < count:
        tokens[filled:] = jnp.zeros((count - filled, width), BF)
        meta[filled:] = jnp.full((count - filled, META), -1.0, BF)

    turned = meta[...].astype(F32).T
    ids, gates = turned[:TOP], turned[TOP : 2 * TOP]
    named, gate = [], []
    for place in range(PLANE):
        expert = (place // NY * NZ + z_ref[0]) * NY + place % NY
        match = ids == expert.astype(F32)
        named.append(jnp.max(jnp.where(match, 1.0, 0.0), axis=0, keepdims=True))
        gate.append(jnp.sum(jnp.where(match, gates, 0.0), axis=0, keepdims=True))
    first = lax.broadcasted_iota(jnp.int32, (count, count), 0)
    second = lax.broadcasted_iota(jnp.int32, (count, count), 1)
    before = (first < second) & (first // ROWS == second // ROWS)
    all_named = jnp.concatenate(named, axis=0)
    rank = jnp.dot(
        all_named.astype(BF), jnp.where(before, 1.0, 0.0).astype(BF), preferred_element_type=F32
    )
    start = (lax.broadcasted_iota(jnp.int32, (1, count), 1) // ROWS + first_block) * CAP
    slot = jnp.where(all_named > 0.0, rank + start.astype(F32), -1.0)
    numbers = (first_slot + lax.broadcasted_iota(jnp.int32, (slots, 1), 0)).astype(F32)
    for pair in range(PLANE // 2):
        hits, weights = [], []
        for place in (2 * pair, 2 * pair + 1):
            hit = slot[place : place + 1] == numbers
            hits.append(jnp.where(hit, 1.0, 0.0))
            weights.append(jnp.where(hit, gate[place], 0.0))
        at = slice(2 * pair * slots, (2 * pair + 2) * slots)
        one_hot[at] = jnp.concatenate(hits, axis=0).astype(BF)
        weight_ref[at] = jnp.concatenate(weights, axis=0).astype(BF)
    tile = 256

    def fill(i, carry):
        at = pl.ds(pl.multiple_of(i * tile, tile), tile)
        out_ref[:, at] = jnp.dot(
            one_hot[...], tokens[:, at], preferred_element_type=F32
        ).astype(BF)
        return carry

    lax.fori_loop(0, width // tile, fill, 0)


def dispatch(blocks, first_block, first_slot, slots, width):
    filled = ROWS * (sum(block.shape[1] for block in blocks) // width)
    count = -(-filled // 128) * 128
    whole = pl.BlockSpec(memory_space=pltpu.VMEM)
    return pl.pallas_call(
        functools.partial(dispatch_body, first_block, first_slot),
        out_shape=(
            jax.ShapeDtypeStruct((PLANE * slots, width), BF),
            jax.ShapeDtypeStruct((PLANE * slots, count), BF),
        ),
        in_specs=[pl.BlockSpec(memory_space=pltpu.SMEM)] + [whole] * len(blocks),
        out_specs=(whole, whole),
        scratch_shapes=[
            pltpu.VMEM((count, width), BF),
            pltpu.VMEM((count, META), BF),
            pltpu.VMEM((PLANE * slots, count), BF),
        ],
        compiler_params=pltpu.CompilerParams(vmem_limit_bytes=24 * 1024 * 1024),
        cost_estimate=pl.CostEstimate(
            flops=2 * PLANE * slots * count * width,
            bytes_accessed=4 * count * width,
            transcendentals=0,
        ),
    )(lax.axis_index("z").astype(jnp.int32).reshape(1), *blocks)


def expert_body(rows_ref, g0, g1, u0, u1, d0, d1, out_ref, g_all, u_all, d_all, hidden, sems):
    half = g0.shape[2]
    copies = [
        pltpu.make_async_copy(g0.at[0], g_all.at[:, :half], sems.at[0]),
        pltpu.make_async_copy(g1.at[0], g_all.at[:, half:], sems.at[1]),
        pltpu.make_async_copy(u0.at[0], u_all.at[:, :half], sems.at[2]),
        pltpu.make_async_copy(u1.at[0], u_all.at[:, half:], sems.at[3]),
        pltpu.make_async_copy(d0.at[0], d_all.at[:half], sems.at[4]),
        pltpu.make_async_copy(d1.at[0], d_all.at[half:], sems.at[5]),
    ]
    for which in (0, 2, 1, 3, 4, 5):
        copies[which].start()
    tile = 256
    for i in range(g_all.shape[1] // tile):
        if i == 0:
            copies[0].wait()
            copies[2].wait()
        if i == half // tile:
            copies[1].wait()
            copies[3].wait()
        at = slice(i * tile, (i + 1) * tile)
        gate_act = jnp.dot(rows_ref[...], g_all[:, at], preferred_element_type=F32)
        up_act = jnp.dot(rows_ref[...], u_all[:, at], preferred_element_type=F32)
        hidden[:, at] = (gate_act / (1.0 + jnp.exp(-gate_act)) * up_act).astype(BF)
    for copy in copies[4:]:
        copy.wait()

    def outer(i, carry):
        at = pl.ds(pl.multiple_of(i * tile, tile), tile)
        out_ref[:, at] = jnp.dot(
            hidden[...], d_all[:, at], preferred_element_type=F32
        ).astype(BF)
        return carry

    lax.fori_loop(0, d_all.shape[1] // tile, outer, 0)


def expert_rows(rows, gate_pair, up_pair, down_pair):
    count, width = rows.shape
    hid = 2 * gate_pair[0].shape[2]
    whole = pl.BlockSpec(memory_space=pltpu.VMEM)
    there = pl.BlockSpec(memory_space=pltpu.HBM)
    return pl.pallas_call(
        expert_body,
        out_shape=jax.ShapeDtypeStruct((count, width), BF),
        in_specs=[whole] + [there] * 6,
        out_specs=whole,
        scratch_shapes=[
            pltpu.VMEM((width, hid), BF),
            pltpu.VMEM((width, hid), BF),
            pltpu.VMEM((hid, width), BF),
            pltpu.VMEM((count, hid), BF),
            pltpu.SemaphoreType.DMA((6,)),
        ],
        compiler_params=pltpu.CompilerParams(vmem_limit_bytes=57 * 1024 * 1024),
        cost_estimate=pl.CostEstimate(
            flops=6 * count * width * hid,
            bytes_accessed=6 * width * hid + 4 * count * width,
            transcendentals=count * hid,
        ),
    )(rows, *gate_pair, *up_pair, *down_pair)


def exchange(rows):
    count, width = rows.shape
    out = lax.all_to_all(
        rows.reshape(PLANE, count // PLANE, width),
        ("x", "y"),
        split_axis=0,
        concat_axis=0,
        tiled=True,
    )
    return out.reshape(count, width)


def weighted_sum(weights, rows):
    return lax.dot_general(weights, rows, (((0,), (0,)), ((), ())), preferred_element_type=F32)


def local(
    queries,
    key_rows,
    value_rows,
    doc_lengths,
    residual_in,
    out_weight,
    norm_gain,
    expert_ids,
    gate_weights,
    w_gate,
    w_up,
    w_down,
):
    pairs = [(w, swap_cores(w)) for w in (w_gate, w_up, w_down)]
    other_weight = swap_cores(out_weight)
    attn_theirs, attn_mine = attend(queries, key_rows, value_rows, doc_lengths)
    attn_theirs, attn_mine, pairs = lax.optimization_barrier((attn_theirs, attn_mine, pairs))
    mid = residual_in.astype(F32) + project(attn_theirs, attn_mine, out_weight, other_weight)
    spread = jnp.mean(mid * mid, axis=1, keepdims=True)
    normed = (mid * lax.rsqrt(spread + 1e-06) * norm_gain[None, :]).astype(BF)

    rows, width = normed.shape
    meta = jnp.concatenate(
        [
            expert_ids.astype(BF),
            gate_weights.astype(BF),
            jnp.zeros((rows, META - 2 * TOP), BF),
        ],
        axis=1,
    )
    blocks = ring_gather(jnp.concatenate([normed, meta], axis=1), width // 2)
    out_near, weight_near = dispatch(blocks[:NEAR], 0, 0, NEAR_SLOTS, width)
    arrived_near = exchange(out_near)
    out_far, weight_far = dispatch(
        blocks[NEAR - 1 :], NEAR - 1, NEAR_SLOTS, SLOTS - NEAR_SLOTS, width
    )
    out_far, arrived_near = lax.optimization_barrier((out_far, arrived_near))
    arrived_far = exchange(out_far)
    pair_near = expert_rows(arrived_near, *pairs)
    arrived_far, pair_near = lax.optimization_barrier((arrived_far, pair_near))
    pair_far = expert_rows(arrived_far, *pairs)

    returned_far = exchange(pair_far)
    returned_far, pair_near = lax.optimization_barrier((returned_far, pair_near))
    returned_near = exchange(pair_near)

    def terms(weights, first, rows):
        picked = weights[:, first * ROWS : (first + 2) * ROWS]
        return weighted_sum(picked, rows).reshape(2, ROWS, width)

    half = width // 2
    to_right, farthest = terms(weight_far, 2, returned_far).astype(BF)
    returned_far, farthest = lax.optimization_barrier((returned_far, farthest))
    right = shift(farthest[:, :half], "z", NZ, 1)
    left = shift(farthest[:, half:], "z", NZ, -1)
    early_right = shift(to_right[:, half:], "z", NZ, 1)
    over, to_left = terms(weight_far, 0, returned_far)
    to_left = to_left.astype(BF)
    early_left = shift(to_left[:, :half], "z", NZ, -1)
    right = shift(add(to_right[:, :half], right), "z", NZ, 1)
    left = shift(add(to_left[:, half:], left), "z", NZ, -1)
    right = jnp.concatenate([right, early_right], axis=1)
    left = jnp.concatenate([early_left, left], axis=1)
    to_left, to_right = terms(weight_near, 2, returned_near).astype(BF)
    right, left = ring_step(right, left, to_right, to_left)
    returned_near = lax.optimization_barrier((returned_near, right, left))[0]
    right, left = shift(right, "z", NZ, 1), shift(left, "z", NZ, -1)
    own, to_left = terms(weight_near, 0, returned_near)
    to_right = terms(weight_near, 4, returned_near)[0] + over
    right, left = ring_step(right, left, to_right.astype(BF), to_left.astype(BF))
    right, left = shift(right, "z", NZ, 1), shift(left, "z", NZ, -1)
    expert_sum = own + right.astype(F32) + left.astype(F32)
    return (mid + expert_sum).astype(BF)


def solution(mesh):
    mesh = Mesh(mesh.devices.reshape(NX, NZ, NY, NC), ("x", "z", "y", "c"))
    seq, head = ("x", "z"), ("y", "c")
    every = seq + head
    placed = (
        P(seq, head),
        P(seq, None),
        P(seq, None),
        P(),
        P(every, None),
        P(head, None),
        P(),
        P(every, None),
        P(every, None),
        P(every, None, None),
        P(every, None, None),
        P(every, None, None),
    )
    return jax.shard_map(
        local, mesh=mesh, in_specs=placed, out_specs=P(every, None), check_vma=False
    )
```

```python
import functools
import math

import jax
import jax.numpy as jnp
from jax import lax
from jax.experimental import pallas as pl
from jax.experimental.pallas import tpu as pltpu
from jax.sharding import Mesh, PartitionSpec as P

HD = 128
NDOCS = 128
NX, NZ, NY, NC = 4, 8, 4, 2
ROWS = 64
CAP = 5
TOP = 8
META = 128
PLANE = NX * NY
SLOTS = NZ * CAP
NEAR = 5
NEAR_SLOTS = 24

BF = jnp.bfloat16
F32 = jnp.float32
masked_low = -1e30

RING = (0, -1, -2, 2, 1, -3, 3, 4)


def shift(value, axis, size, by):
    return lax.ppermute(value, axis, [(i, (i + by) % size) for i in range(size)])


def swap_cores(value):
    return lax.ppermute(value, "c", [(0, 1), (1, 0)])


def from_behind(value):
    devices = NX * NZ
    return lax.ppermute(value, ("x", "z"), [(i, i + 1) for i in range(devices - 1)])


def attend_half(base, queries, keys, values, lengths, store):
    rows = queries.shape[0]
    place = lax.broadcasted_iota(jnp.int32, (NDOCS, NDOCS), 0)
    upto = place <= lax.broadcasted_iota(jnp.int32, (NDOCS, NDOCS), 1)
    spread = jnp.broadcast_to(lengths.astype(F32), (8, NDOCS)).astype(BF)
    ends = jnp.dot(spread, jnp.where(upto, 1.0, 0.0).astype(BF), preferred_element_type=F32)[:1]
    query_pos = base + lax.broadcasted_iota(jnp.int32, (rows, 1), 0)
    ended = ends <= query_pos.astype(F32)
    start = jnp.max(jnp.where(ended, ends, 0.0), axis=1, keepdims=True).astype(jnp.int32)
    span = 2 * keys[0].shape[0]
    key_pos = base - keys[0].shape[0] + lax.broadcasted_iota(jnp.int32, (1, span), 1)
    visible = (key_pos <= query_pos) & (key_pos >= start)
    key_window = jnp.concatenate(keys, axis=0)
    value_window = jnp.concatenate(values, axis=0)
    for head in range(queries.shape[1] // HD):
        at = slice(head * HD, (head + 1) * HD)
        scores = lax.dot_general(
            queries[:, at], key_window, (((1,), (1,)), ((), ())), preferred_element_type=F32
        ) * (1.0 / math.sqrt(HD))
        scores = jnp.where(visible, scores, masked_low)
        weights = jnp.exp(scores - jnp.max(scores, axis=1, keepdims=True))
        total = jnp.sum(weights, axis=1, keepdims=True)
        mixture = jnp.dot(weights.astype(BF), value_window, preferred_element_type=F32)
        store(at, (mixture / total).astype(BF))


def late_body(where, q_ref, ka, kb, va, vb, len_ref, out_ref):
    def store(at, value):
        out_ref[:, at] = value

    attend_half(
        where[0] + q_ref.shape[0], q_ref[...], [ka[...], kb[...]], [va[...], vb[...]], len_ref[...], store
    )


def early_body(where, q_ref, tails, kb, vb, len_ref, late_ref, theirs_ref, mine_ref, held):
    rows = q_ref.shape[0]

    def store(at, value):
        held[:rows, at] = value

    held[rows:] = late_ref[...]
    attend_half(
        where[0], q_ref[...], [tails[0], kb[...]], [tails[1], vb[...]], len_ref[...], store
    )
    y, c = where[1], where[2]
    for k in range(NY):
        block = lax.rem(y + k, NY) * (NC * ROWS)
        here = pl.ds(pl.multiple_of(block + c * ROWS, ROWS), ROWS)
        there = pl.ds(pl.multiple_of(block + (1 - c) * ROWS, ROWS), ROWS)
        mine_ref[k * ROWS : (k + 1) * ROWS] = held[here]
        theirs_ref[k * ROWS : (k + 1) * ROWS] = held[there]


def attend(queries, key_rows, value_rows, doc_lengths):
    tok_rows, width = queries.shape
    half = tok_rows // 2
    y, c = lax.axis_index("y"), lax.axis_index("c")
    where = jnp.stack([lax.axis_index(("x", "z")) * tok_rows, y, c]).astype(jnp.int32)
    lengths = doc_lengths.reshape(1, -1)
    tails = from_behind(
        jnp.stack(
            [
                lax.dynamic_slice(rows, (half, y * HD), (half, HD))
                for rows in (key_rows, value_rows)
            ]
        )
    )

    def part(i):
        return pl.BlockSpec((half, HD), lambda g, where: (i, where[1]))

    def all_of(*shape):
        return pl.BlockSpec(shape, lambda g, where: (0,) * len(shape))

    lens = all_of(1, doc_lengths.shape[0])
    params = pltpu.CompilerParams(vmem_limit_bytes=57 * 1024 * 1024)
    scores = tok_rows * tok_rows * (width // HD) // 2
    late = pl.pallas_call(
        late_body,
        out_shape=jax.ShapeDtypeStruct((half, width), BF),
        grid_spec=pltpu.PrefetchScalarGridSpec(
            num_scalar_prefetch=1,
            grid=(1,),
            in_specs=[
                pl.BlockSpec((half, width), lambda g, where: (1, 0)),
                part(0),
                part(1),
                part(0),
                part(1),
                lens,
            ],
            out_specs=all_of(half, width),
        ),
        compiler_params=params,
        cost_estimate=pl.CostEstimate(
            flops=16 * scores * HD, bytes_accessed=6 * half * width, transcendentals=8 * scores
        ),
    )(where, queries, key_rows, key_rows, value_rows, value_rows, lengths)
    return pl.pallas_call(
        early_body,
        out_shape=(
            jax.ShapeDtypeStruct((half, width), BF),
            jax.ShapeDtypeStruct((half, width), BF),
        ),
        grid_spec=pltpu.PrefetchScalarGridSpec(
            num_scalar_prefetch=1,
            grid=(1,),
            in_specs=[
                pl.BlockSpec((half, width), lambda g, where: (0, 0)),
                all_of(2, half, HD),
                part(0),
                part(0),
                lens,
                all_of(half, width),
            ],
            out_specs=(all_of(half, width), all_of(half, width)),
            scratch_shapes=[pltpu.VMEM((tok_rows, width), BF)],
        ),
        compiler_params=params,
        cost_estimate=pl.CostEstimate(
            flops=16 * scores * HD, bytes_accessed=8 * half * width, transcendentals=8 * scores
        ),
    )(where, queries, tails, key_rows, value_rows, lengths, late)


def project(attn_theirs, attn_mine, out_weight, other_weight):
    arrived = swap_cores(attn_theirs)
    mine = lax.optimization_barrier(
        jnp.dot(attn_mine, out_weight, preferred_element_type=F32)
    )
    both = mine + jnp.dot(arrived, other_weight, preferred_element_type=F32)
    both = both.reshape(NY, ROWS, out_weight.shape[1])
    sent = both.astype(BF)
    moved = [shift(sent[k], "y", NY, k) for k in range(1, NY)]
    return both[0] + sum(block.astype(F32) for block in moved)


def ring_gather(own, half):
    parts = [own[:, :half], own[:, half:]]
    blocks = {0: parts}
    right, left = parts, parts
    for hops in (1, 2, 3):
        right = blocks[-hops] = [shift(part, "z", NZ, 1) for part in right]
        left = blocks[hops] = [shift(part, "z", NZ, -1) for part in left]
    blocks[4] = [shift(right[0], "z", NZ, 1), shift(left[1], "z", NZ, -1)]
    return [part for offset in RING for part in blocks[offset]]


def add(a, b):
    return (a.astype(F32) + b.astype(F32)).astype(BF)


def ring_step(right, left, to_right, to_left):
    half = right[0].shape[1]
    plan = [
        (right[1], to_right[:, half:], 1),
        (left[0], to_left[:, :half], -1),
        (right[0], to_right[:, :half], 1),
        (left[1], to_left[:, half:], -1),
    ]
    sent, last = [], None
    for value, own, by in plan:
        if last is not None:
            own = lax.optimization_barrier((own, last))[0]
        last = add(value, own)
        sent.append(shift(last, "z", NZ, by))
    return (sent[2], sent[0]), (sent[1], sent[3]), last


def dispatch_body(first_block, first_slot, z_ref, *refs):
    blocks, (out_ref, weight_ref, tokens, meta, one_hot) = refs[:-5], refs[-5:]
    count, width = tokens.shape
    slots = out_ref.shape[0] // PLANE
    filled = 0
    column = 0
    for block in blocks:
        at = slice(filled, filled + ROWS)
        here = min(block.shape[1], width - column)
        tokens[at, column : column + here] = block[:, :here]
        column += here
        if block.shape[1] > here:
            meta[at] = block[:, here:]
        if column == width:
            filled, column = filled + ROWS, 0
    if filled < count:
        tokens[filled:] = jnp.zeros((count - filled, width), BF)
        meta[filled:] = jnp.full((count - filled, META), -1.0, BF)

    turned = meta[...].astype(F32).T
    ids, gates = turned[:TOP], turned[TOP : 2 * TOP]
    named, gate = [], []
    for place in range(PLANE):
        expert = (place // NY * NZ + z_ref[0]) * NY + place % NY
        match = ids == expert.astype(F32)
        named.append(jnp.max(jnp.where(match, 1.0, 0.0), axis=0, keepdims=True))
        gate.append(jnp.sum(jnp.where(match, gates, 0.0), axis=0, keepdims=True))
    first = lax.broadcasted_iota(jnp.int32, (count, count), 0)
    second = lax.broadcasted_iota(jnp.int32, (count, count), 1)
    before = (first < second) & (first // ROWS == second // ROWS)
    all_named = jnp.concatenate(named, axis=0)
    rank = jnp.dot(
        all_named.astype(BF), jnp.where(before, 1.0, 0.0).astype(BF), preferred_element_type=F32
    )
    start = (lax.broadcasted_iota(jnp.int32, (1, count), 1) // ROWS + first_block) * CAP
    slot = jnp.where(all_named > 0.0, rank + start.astype(F32), -1.0)
    numbers = (first_slot + lax.broadcasted_iota(jnp.int32, (slots, 1), 0)).astype(F32)
    for pair in range(PLANE // 2):
        hits, weights = [], []
        for place in (2 * pair, 2 * pair + 1):
            hit = slot[place : place + 1] == numbers
            hits.append(jnp.where(hit, 1.0, 0.0))
            weights.append(jnp.where(hit, gate[place], 0.0))
        at = slice(2 * pair * slots, (2 * pair + 2) * slots)
        one_hot[at] = jnp.concatenate(hits, axis=0).astype(BF)
        weight_ref[at] = jnp.concatenate(weights, axis=0).astype(BF)
    tile = 256

    def fill(i, carry):
        at = pl.ds(pl.multiple_of(i * tile, tile), tile)
        out_ref[:, at] = jnp.dot(
            one_hot[...], tokens[:, at], preferred_element_type=F32
        ).astype(BF)
        return carry

    lax.fori_loop(0, width // tile, fill, 0)


def dispatch(blocks, first_block, first_slot, slots, width):
    filled = ROWS * (sum(block.shape[1] for block in blocks) // width)
    count = -(-filled // 128) * 128
    whole = pl.BlockSpec(memory_space=pltpu.VMEM)
    return pl.pallas_call(
        functools.partial(dispatch_body, first_block, first_slot),
        out_shape=(
            jax.ShapeDtypeStruct((PLANE * slots, width), BF),
            jax.ShapeDtypeStruct((PLANE * slots, count), BF),
        ),
        in_specs=[pl.BlockSpec(memory_space=pltpu.SMEM)] + [whole] * len(blocks),
        out_specs=(whole, whole),
        scratch_shapes=[
            pltpu.VMEM((count, width), BF),
            pltpu.VMEM((count, META), BF),
            pltpu.VMEM((PLANE * slots, count), BF),
        ],
        compiler_params=pltpu.CompilerParams(vmem_limit_bytes=24 * 1024 * 1024),
        cost_estimate=pl.CostEstimate(
            flops=2 * PLANE * slots * count * width,
            bytes_accessed=4 * count * width,
            transcendentals=0,
        ),
    )(lax.axis_index("z").astype(jnp.int32).reshape(1), *blocks)


def expert_body(rows_ref, g0, g1, u0, u1, d0, d1, out_ref, g_all, u_all, d_all, hidden, sems):
    half = g0.shape[2]
    copies = [
        pltpu.make_async_copy(g0.at[0], g_all.at[:, :half], sems.at[0]),
        pltpu.make_async_copy(g1.at[0], g_all.at[:, half:], sems.at[1]),
        pltpu.make_async_copy(u0.at[0], u_all.at[:, :half], sems.at[2]),
        pltpu.make_async_copy(u1.at[0], u_all.at[:, half:], sems.at[3]),
        pltpu.make_async_copy(d0.at[0], d_all.at[:half], sems.at[4]),
        pltpu.make_async_copy(d1.at[0], d_all.at[half:], sems.at[5]),
    ]
    for which in (0, 2, 1, 3, 4, 5):
        copies[which].start()
    tile = 256
    for i in range(g_all.shape[1] // tile):
        if i == 0:
            copies[0].wait()
            copies[2].wait()
        if i == half // tile:
            copies[1].wait()
            copies[3].wait()
        at = slice(i * tile, (i + 1) * tile)
        gate_act = jnp.dot(rows_ref[...], g_all[:, at], preferred_element_type=F32)
        up_act = jnp.dot(rows_ref[...], u_all[:, at], preferred_element_type=F32)
        hidden[:, at] = (gate_act / (1.0 + jnp.exp(-gate_act)) * up_act).astype(BF)
    for copy in copies[4:]:
        copy.wait()

    def outer(i, carry):
        at = pl.ds(pl.multiple_of(i * tile, tile), tile)
        out_ref[:, at] = jnp.dot(
            hidden[...], d_all[:, at], preferred_element_type=F32
        ).astype(BF)
        return carry

    lax.fori_loop(0, d_all.shape[1] // tile, outer, 0)


def expert_rows(rows, gate_pair, up_pair, down_pair):
    count, width = rows.shape
    hid = 2 * gate_pair[0].shape[2]
    whole = pl.BlockSpec(memory_space=pltpu.VMEM)
    there = pl.BlockSpec(memory_space=pltpu.HBM)
    return pl.pallas_call(
        expert_body,
        out_shape=jax.ShapeDtypeStruct((count, width), BF),
        in_specs=[whole] + [there] * 6,
        out_specs=whole,
        scratch_shapes=[
            pltpu.VMEM((width, hid), BF),
            pltpu.VMEM((width, hid), BF),
            pltpu.VMEM((hid, width), BF),
            pltpu.VMEM((count, hid), BF),
            pltpu.SemaphoreType.DMA((6,)),
        ],
        compiler_params=pltpu.CompilerParams(vmem_limit_bytes=57 * 1024 * 1024),
        cost_estimate=pl.CostEstimate(
            flops=6 * count * width * hid,
            bytes_accessed=6 * width * hid + 4 * count * width,
            transcendentals=count * hid,
        ),
    )(rows, *gate_pair, *up_pair, *down_pair)


def exchange(rows):
    count, width = rows.shape
    out = lax.all_to_all(
        rows.reshape(PLANE, count // PLANE, width),
        ("x", "y"),
        split_axis=0,
        concat_axis=0,
        tiled=True,
    )
    return out.reshape(count, width)


def weighted_sum(weights, rows):
    return lax.dot_general(weights, rows, (((0,), (0,)), ((), ())), preferred_element_type=F32)


def local(
    queries,
    key_rows,
    value_rows,
    doc_lengths,
    residual_in,
    out_weight,
    norm_gain,
    expert_ids,
    gate_weights,
    w_gate,
    w_up,
    w_down,
):
    pairs = [(w, swap_cores(w)) for w in (w_gate, w_up, w_down)]
    other_weight = swap_cores(out_weight)
    attn_theirs, attn_mine = attend(queries, key_rows, value_rows, doc_lengths)
    attn_theirs, attn_mine, pairs = lax.optimization_barrier((attn_theirs, attn_mine, pairs))
    mid = residual_in.astype(F32) + project(attn_theirs, attn_mine, out_weight, other_weight)
    spread = jnp.mean(mid * mid, axis=1, keepdims=True)
    normed = (mid * lax.rsqrt(spread + 1e-06) * norm_gain[None, :]).astype(BF)

    rows, width = normed.shape
    meta = jnp.concatenate(
        [
            expert_ids.astype(BF),
            gate_weights.astype(BF),
            jnp.zeros((rows, META - 2 * TOP), BF),
        ],
        axis=1,
    )
    blocks = ring_gather(jnp.concatenate([normed, meta], axis=1), width // 2)
    out_near, weight_near = dispatch(blocks[: 2 * NEAR], 0, 0, NEAR_SLOTS, width)
    arrived_near = exchange(out_near)
    out_far, weight_far = dispatch(
        blocks[2 * NEAR - 2 :], NEAR - 1, NEAR_SLOTS, SLOTS - NEAR_SLOTS, width
    )
    out_far, arrived_near = lax.optimization_barrier((out_far, arrived_near))
    arrived_far = exchange(out_far)
    pair_near = expert_rows(arrived_near, *pairs)
    arrived_far, pair_near = lax.optimization_barrier((arrived_far, pair_near))
    pair_far = expert_rows(arrived_far, *pairs)

    returned_far = exchange(pair_far)
    returned_far, pair_near = lax.optimization_barrier((returned_far, pair_near))
    returned_near = exchange(pair_near)

    def terms(weights, first, rows):
        picked = weights[:, first * ROWS : (first + 2) * ROWS]
        return weighted_sum(picked, rows).reshape(2, ROWS, width)

    half = width // 2
    to_right, farthest = terms(weight_far, 2, returned_far).astype(BF)
    returned_far, farthest = lax.optimization_barrier((returned_far, farthest))
    right = shift(farthest[:, :half], "z", NZ, 1)
    left = shift(farthest[:, half:], "z", NZ, -1)
    early_right = shift(to_right[:, half:], "z", NZ, 1)
    over, to_left = terms(weight_far, 0, returned_far)
    to_left = to_left.astype(BF)
    early_left = shift(to_left[:, :half], "z", NZ, -1)
    right = shift(add(to_right[:, :half], right), "z", NZ, 1)
    left = shift(add(to_left[:, half:], left), "z", NZ, -1)
    right, left = (right, early_right), (early_left, left)
    to_left, to_right = terms(weight_near, 2, returned_near).astype(BF)
    right, left, last = ring_step(right, left, to_right, to_left)
    returned_near = lax.optimization_barrier((returned_near, last))[0]
    own, to_left = terms(weight_near, 0, returned_near)
    to_right = terms(weight_near, 4, returned_near)[0] + over
    right, left, _ = ring_step(right, left, to_right.astype(BF), to_left.astype(BF))
    expert_sum = own + sum(jnp.concatenate(way, axis=1).astype(F32) for way in (right, left))
    return (mid + expert_sum).astype(BF)


def solution(mesh):
    mesh = Mesh(mesh.devices.reshape(NX, NZ, NY, NC), ("x", "z", "y", "c"))
    seq, head = ("x", "z"), ("y", "c")
    every = seq + head
    placed = (
        P(seq, head),
        P(seq, None),
        P(seq, None),
        P(),
        P(every, None),
        P(head, None),
        P(),
        P(every, None),
        P(every, None),
        P(every, None, None),
        P(every, None, None),
        P(every, None, None),
    )
    return jax.shard_map(
        local, mesh=mesh, in_specs=placed, out_specs=P(every, None), check_vma=False
    )
```

```python
import functools
import math

import jax
import jax.numpy as jnp
from jax import lax
from jax.experimental import pallas as pl
from jax.experimental.pallas import tpu as pltpu
from jax.sharding import Mesh, PartitionSpec as P

HD = 128
NDOCS = 128
NX, NZ, NY, NC = 4, 8, 4, 2
ROWS = 64
CAP = 5
TOP = 8
META = 128
PLANE = NX * NY
SLOTS = NZ * CAP
NEAR = 5
NEAR_SLOTS = 24

BF = jnp.bfloat16
F32 = jnp.float32
masked_low = -1e30

RING = (0, -1, -2, 2, 1, -3, 3, 4)


def shift(value, axis, size, by):
    return lax.ppermute(value, axis, [(i, (i + by) % size) for i in range(size)])


def swap_cores(value):
    return lax.ppermute(value, "c", [(0, 1), (1, 0)])


def from_behind(value):
    devices = NX * NZ
    return lax.ppermute(value, ("x", "z"), [(i, i + 1) for i in range(devices - 1)])


def attend_half(base, queries, keys, values, lengths, store):
    rows = queries.shape[0]
    place = lax.broadcasted_iota(jnp.int32, (NDOCS, NDOCS), 0)
    upto = place <= lax.broadcasted_iota(jnp.int32, (NDOCS, NDOCS), 1)
    spread = jnp.broadcast_to(lengths.astype(F32), (8, NDOCS)).astype(BF)
    ends = jnp.dot(spread, jnp.where(upto, 1.0, 0.0).astype(BF), preferred_element_type=F32)[:1]
    query_pos = base + lax.broadcasted_iota(jnp.int32, (rows, 1), 0)
    ended = ends <= query_pos.astype(F32)
    start = jnp.max(jnp.where(ended, ends, 0.0), axis=1, keepdims=True).astype(jnp.int32)
    span = 2 * keys[0].shape[0]
    key_pos = base - keys[0].shape[0] + lax.broadcasted_iota(jnp.int32, (1, span), 1)
    visible = (key_pos <= query_pos) & (key_pos >= start)
    key_window = jnp.concatenate(keys, axis=0)
    value_window = jnp.concatenate(values, axis=0)
    for head in range(queries.shape[1] // HD):
        at = slice(head * HD, (head + 1) * HD)
        scores = lax.dot_general(
            queries[:, at], key_window, (((1,), (1,)), ((), ())), preferred_element_type=F32
        ) * (1.0 / math.sqrt(HD))
        scores = jnp.where(visible, scores, masked_low)
        weights = jnp.exp(scores - jnp.max(scores, axis=1, keepdims=True))
        total = jnp.sum(weights, axis=1, keepdims=True)
        mixture = jnp.dot(weights.astype(BF), value_window, preferred_element_type=F32)
        store(at, (mixture / total).astype(BF))


def late_body(where, q_ref, ka, kb, va, vb, len_ref, out_ref):
    def store(at, value):
        out_ref[:, at] = value

    attend_half(
        where[0] + q_ref.shape[0], q_ref[...], [ka[...], kb[...]], [va[...], vb[...]], len_ref[...], store
    )


def early_body(where, q_ref, tails, kb, vb, len_ref, late_ref, theirs_ref, mine_ref, held):
    rows = q_ref.shape[0]

    def store(at, value):
        held[:rows, at] = value

    held[rows:] = late_ref[...]
    attend_half(
        where[0], q_ref[...], [tails[0], kb[...]], [tails[1], vb[...]], len_ref[...], store
    )
    y, c = where[1], where[2]
    for k in range(NY):
        block = lax.rem(y + k, NY) * (NC * ROWS)
        here = pl.ds(pl.multiple_of(block + c * ROWS, ROWS), ROWS)
        there = pl.ds(pl.multiple_of(block + (1 - c) * ROWS, ROWS), ROWS)
        mine_ref[k * ROWS : (k + 1) * ROWS] = held[here]
        theirs_ref[k * ROWS : (k + 1) * ROWS] = held[there]


def attend(queries, key_rows, value_rows, doc_lengths):
    tok_rows, width = queries.shape
    half = tok_rows // 2
    y, c = lax.axis_index("y"), lax.axis_index("c")
    where = jnp.stack([lax.axis_index(("x", "z")) * tok_rows, y, c]).astype(jnp.int32)
    lengths = doc_lengths.reshape(1, -1)
    tails = from_behind(
        jnp.stack(
            [
                lax.dynamic_slice(rows, (half, y * HD), (half, HD))
                for rows in (key_rows, value_rows)
            ]
        )
    )

    def part(i):
        return pl.BlockSpec((half, HD), lambda g, where: (i, where[1]))

    def all_of(*shape):
        return pl.BlockSpec(shape, lambda g, where: (0,) * len(shape))

    lens = all_of(1, doc_lengths.shape[0])
    params = pltpu.CompilerParams(vmem_limit_bytes=57 * 1024 * 1024)
    scores = tok_rows * tok_rows * (width // HD) // 2
    late = pl.pallas_call(
        late_body,
        out_shape=jax.ShapeDtypeStruct((half, width), BF),
        grid_spec=pltpu.PrefetchScalarGridSpec(
            num_scalar_prefetch=1,
            grid=(1,),
            in_specs=[
                pl.BlockSpec((half, width), lambda g, where: (1, 0)),
                part(0),
                part(1),
                part(0),
                part(1),
                lens,
            ],
            out_specs=all_of(half, width),
        ),
        compiler_params=params,
        cost_estimate=pl.CostEstimate(
            flops=16 * scores * HD, bytes_accessed=6 * half * width, transcendentals=8 * scores
        ),
    )(where, queries, key_rows, key_rows, value_rows, value_rows, lengths)
    return pl.pallas_call(
        early_body,
        out_shape=(
            jax.ShapeDtypeStruct((half, width), BF),
            jax.ShapeDtypeStruct((half, width), BF),
        ),
        grid_spec=pltpu.PrefetchScalarGridSpec(
            num_scalar_prefetch=1,
            grid=(1,),
            in_specs=[
                pl.BlockSpec((half, width), lambda g, where: (0, 0)),
                all_of(2, half, HD),
                part(0),
                part(0),
                lens,
                all_of(half, width),
            ],
            out_specs=(all_of(half, width), all_of(half, width)),
            scratch_shapes=[pltpu.VMEM((tok_rows, width), BF)],
        ),
        compiler_params=params,
        cost_estimate=pl.CostEstimate(
            flops=16 * scores * HD, bytes_accessed=8 * half * width, transcendentals=8 * scores
        ),
    )(where, queries, tails, key_rows, value_rows, lengths, late)


def project(attn_theirs, attn_mine, out_weight, other_weight):
    arrived = swap_cores(attn_theirs)
    mine = lax.optimization_barrier(
        jnp.dot(attn_mine, out_weight, preferred_element_type=F32)
    )
    both = mine + jnp.dot(arrived, other_weight, preferred_element_type=F32)
    both = both.reshape(NY, ROWS, out_weight.shape[1])
    sent = both.astype(BF)
    moved = [shift(sent[k], "y", NY, k) for k in (2, 1, 3)]
    return both[0] + sum(block.astype(F32) for block in moved)


def ring_gather(own, half):
    blocks = {0: own}
    right = left = own
    for hops in (1, 2, 3):
        right = blocks[-hops] = shift(right, "z", NZ, 1)
        left = blocks[hops] = shift(left, "z", NZ, -1)
    last = [shift(right[:, :half], "z", NZ, 1), shift(left[:, half:], "z", NZ, -1)]
    return [blocks[offset] for offset in RING[:-1]] + last


def add(a, b):
    return (a.astype(F32) + b.astype(F32)).astype(BF)


def ring_step(right, left, to_right, to_left):
    right = add(right, to_right)
    to_left = lax.optimization_barrier((to_left, right))[0]
    left = add(left, to_left)
    return right, left


def dispatch_body(first_block, first_slot, z_ref, *refs):
    blocks, (out_ref, weight_ref, tokens, meta, one_hot) = refs[:-5], refs[-5:]
    count, width = tokens.shape
    slots = out_ref.shape[0] // PLANE
    filled = 0
    column = 0
    for block in blocks:
        at = slice(filled, filled + ROWS)
        here = min(block.shape[1], width - column)
        tokens[at, column : column + here] = block[:, :here]
        column += here
        if block.shape[1] > here:
            meta[at] = block[:, here:]
        if column == width:
            filled, column = filled + ROWS, 0
    if filled < count:
        tokens[filled:] = jnp.zeros((count - filled, width), BF)
        meta[filled:] = jnp.full((count - filled, META), -1.0, BF)

    turned = meta[...].astype(F32).T
    ids, gates = turned[:TOP], turned[TOP : 2 * TOP]
    named, gate = [], []
    for place in range(PLANE):
        expert = (place // NY * NZ + z_ref[0]) * NY + place % NY
        match = ids == expert.astype(F32)
        named.append(jnp.max(jnp.where(match, 1.0, 0.0), axis=0, keepdims=True))
        gate.append(jnp.sum(jnp.where(match, gates, 0.0), axis=0, keepdims=True))
    first = lax.broadcasted_iota(jnp.int32, (count, count), 0)
    second = lax.broadcasted_iota(jnp.int32, (count, count), 1)
    before = (first < second) & (first // ROWS == second // ROWS)
    all_named = jnp.concatenate(named, axis=0)
    rank = jnp.dot(
        all_named.astype(BF), jnp.where(before, 1.0, 0.0).astype(BF), preferred_element_type=F32
    )
    start = (lax.broadcasted_iota(jnp.int32, (1, count), 1) // ROWS + first_block) * CAP
    slot = jnp.where(all_named > 0.0, rank + start.astype(F32), -1.0)
    numbers = (first_slot + lax.broadcasted_iota(jnp.int32, (slots, 1), 0)).astype(F32)
    for pair in range(PLANE // 2):
        hits, weights = [], []
        for place in (2 * pair, 2 * pair + 1):
            hit = slot[place : place + 1] == numbers
            hits.append(jnp.where(hit, 1.0, 0.0))
            weights.append(jnp.where(hit, gate[place], 0.0))
        at = slice(2 * pair * slots, (2 * pair + 2) * slots)
        one_hot[at] = jnp.concatenate(hits, axis=0).astype(BF)
        weight_ref[at] = jnp.concatenate(weights, axis=0).astype(BF)
    tile = 256

    def fill(i, carry):
        at = pl.ds(pl.multiple_of(i * tile, tile), tile)
        out_ref[:, at] = jnp.dot(
            one_hot[...], tokens[:, at], preferred_element_type=F32
        ).astype(BF)
        return carry

    lax.fori_loop(0, width // tile, fill, 0)


def dispatch(blocks, first_block, first_slot, slots, width):
    filled = ROWS * (sum(block.shape[1] for block in blocks) // width)
    count = -(-filled // 128) * 128
    whole = pl.BlockSpec(memory_space=pltpu.VMEM)
    return pl.pallas_call(
        functools.partial(dispatch_body, first_block, first_slot),
        out_shape=(
            jax.ShapeDtypeStruct((PLANE * slots, width), BF),
            jax.ShapeDtypeStruct((PLANE * slots, count), BF),
        ),
        in_specs=[pl.BlockSpec(memory_space=pltpu.SMEM)] + [whole] * len(blocks),
        out_specs=(whole, whole),
        scratch_shapes=[
            pltpu.VMEM((count, width), BF),
            pltpu.VMEM((count, META), BF),
            pltpu.VMEM((PLANE * slots, count), BF),
        ],
        compiler_params=pltpu.CompilerParams(vmem_limit_bytes=24 * 1024 * 1024),
        cost_estimate=pl.CostEstimate(
            flops=2 * PLANE * slots * count * width,
            bytes_accessed=4 * count * width,
            transcendentals=0,
        ),
    )(lax.axis_index("z").astype(jnp.int32).reshape(1), *blocks)


def expert_body(rows_ref, g0, g1, u0, u1, d0, d1, out_ref, g_all, u_all, d_all, hidden, sems):
    half = g0.shape[2]
    copies = [
        pltpu.make_async_copy(g0.at[0], g_all.at[:, :half], sems.at[0]),
        pltpu.make_async_copy(g1.at[0], g_all.at[:, half:], sems.at[1]),
        pltpu.make_async_copy(u0.at[0], u_all.at[:, :half], sems.at[2]),
        pltpu.make_async_copy(u1.at[0], u_all.at[:, half:], sems.at[3]),
        pltpu.make_async_copy(d0.at[0], d_all.at[:half], sems.at[4]),
        pltpu.make_async_copy(d1.at[0], d_all.at[half:], sems.at[5]),
    ]
    for which in (0, 2, 1, 3, 4, 5):
        copies[which].start()
    tile = 256
    for i in range(g_all.shape[1] // tile):
        if i == 0:
            copies[0].wait()
            copies[2].wait()
        if i == half // tile:
            copies[1].wait()
            copies[3].wait()
        at = slice(i * tile, (i + 1) * tile)
        gate_act = jnp.dot(rows_ref[...], g_all[:, at], preferred_element_type=F32)
        up_act = jnp.dot(rows_ref[...], u_all[:, at], preferred_element_type=F32)
        hidden[:, at] = (gate_act / (1.0 + jnp.exp(-gate_act)) * up_act).astype(BF)
    for copy in copies[4:]:
        copy.wait()

    def outer(i, carry):
        at = pl.ds(pl.multiple_of(i * tile, tile), tile)
        out_ref[:, at] = jnp.dot(
            hidden[...], d_all[:, at], preferred_element_type=F32
        ).astype(BF)
        return carry

    lax.fori_loop(0, d_all.shape[1] // tile, outer, 0)


def expert_rows(rows, gate_pair, up_pair, down_pair, limit=57):
    count, width = rows.shape
    hid = 2 * gate_pair[0].shape[2]
    whole = pl.BlockSpec(memory_space=pltpu.VMEM)
    there = pl.BlockSpec(memory_space=pltpu.HBM)
    return pl.pallas_call(
        expert_body,
        out_shape=jax.ShapeDtypeStruct((count, width), BF),
        in_specs=[whole] + [there] * 6,
        out_specs=whole,
        scratch_shapes=[
            pltpu.VMEM((width, hid), BF),
            pltpu.VMEM((width, hid), BF),
            pltpu.VMEM((hid, width), BF),
            pltpu.VMEM((count, hid), BF),
            pltpu.SemaphoreType.DMA((6,)),
        ],
        compiler_params=pltpu.CompilerParams(vmem_limit_bytes=limit * 1024 * 1024),
        cost_estimate=pl.CostEstimate(
            flops=6 * count * width * hid,
            bytes_accessed=6 * width * hid + 4 * count * width,
            transcendentals=count * hid,
        ),
    )(rows, *gate_pair, *up_pair, *down_pair)


def exchange(rows):
    count, width = rows.shape
    out = lax.all_to_all(
        rows.reshape(PLANE, count // PLANE, width),
        ("x", "y"),
        split_axis=0,
        concat_axis=0,
        tiled=True,
    )
    return out.reshape(count, width)


def weighted_sum(weights, rows):
    return lax.dot_general(weights, rows, (((0,), (0,)), ((), ())), preferred_element_type=F32)


def local(
    queries,
    key_rows,
    value_rows,
    doc_lengths,
    residual_in,
    out_weight,
    norm_gain,
    expert_ids,
    gate_weights,
    w_gate,
    w_up,
    w_down,
):
    pairs = [(w, swap_cores(w)) for w in (w_gate, w_up, w_down)]
    other_weight = swap_cores(out_weight)
    attn_theirs, attn_mine = attend(queries, key_rows, value_rows, doc_lengths)
    attn_theirs, attn_mine, pairs = lax.optimization_barrier((attn_theirs, attn_mine, pairs))
    mid = residual_in.astype(F32) + project(attn_theirs, attn_mine, out_weight, other_weight)
    mid = lax.optimization_barrier(mid)
    spread = jnp.mean(mid * mid, axis=1, keepdims=True)
    normed = (mid * lax.rsqrt(spread + 1e-06) * norm_gain[None, :]).astype(BF)

    rows, width = normed.shape
    meta = jnp.concatenate(
        [
            expert_ids.astype(BF),
            gate_weights.astype(BF),
            jnp.zeros((rows, META - 2 * TOP), BF),
        ],
        axis=1,
    )
    blocks = ring_gather(jnp.concatenate([normed, meta], axis=1), width // 2)
    out_near, weight_near = dispatch(blocks[:NEAR], 0, 0, NEAR_SLOTS, width)
    arrived_near = exchange(out_near)
    out_far, weight_far = dispatch(
        blocks[NEAR - 1 :], NEAR - 1, NEAR_SLOTS, SLOTS - NEAR_SLOTS, width
    )
    out_far, arrived_near = lax.optimization_barrier((out_far, arrived_near))
    arrived_far = exchange(out_far)
    pair_near = expert_rows(arrived_near, *pairs)
    arrived_far, pair_near = lax.optimization_barrier((arrived_far, pair_near))
    pair_far = expert_rows(arrived_far, *pairs, limit=52)

    returned_far = exchange(pair_far)
    returned_far, pair_near = lax.optimization_barrier((returned_far, pair_near))
    returned_near = exchange(pair_near)

    def terms(weights, first, rows):
        picked = weights[:, first * ROWS : (first + 2) * ROWS]
        return weighted_sum(picked, rows).reshape(2, ROWS, width)

    half = width // 2
    to_right, farthest = terms(weight_far, 2, returned_far).astype(BF)
    returned_far, farthest = lax.optimization_barrier((returned_far, farthest))
    right = shift(farthest[:, :half], "z", NZ, 1)
    left = shift(farthest[:, half:], "z", NZ, -1)
    early_right = shift(to_right[:, half:], "z", NZ, 1)
    over, to_left = terms(weight_far, 0, returned_far)
    to_left = to_left.astype(BF)
    early_left = shift(to_left[:, :half], "z", NZ, -1)
    right = shift(add(to_right[:, :half], right), "z", NZ, 1)
    left = shift(add(to_left[:, half:], left), "z", NZ, -1)
    right = jnp.concatenate([right, early_right], axis=1)
    left = jnp.concatenate([early_left, left], axis=1)
    to_left, to_right = terms(weight_near, 2, returned_near).astype(BF)
    right, left = ring_step(right, left, to_right, to_left)
    returned_near = lax.optimization_barrier((returned_near, right, left))[0]
    right, left = shift(right, "z", NZ, 1), shift(left, "z", NZ, -1)
    own, to_left = terms(weight_near, 0, returned_near)
    to_right = terms(weight_near, 4, returned_near)[0] + over
    right, left = ring_step(right, left, to_right.astype(BF), to_left.astype(BF))
    right, left = shift(right, "z", NZ, 1), shift(left, "z", NZ, -1)
    expert_sum = own + right.astype(F32) + left.astype(F32)
    return (mid + expert_sum).astype(BF)


def solution(mesh):
    mesh = Mesh(mesh.devices.reshape(NX, NZ, NY, NC), ("x", "z", "y", "c"))
    seq, head = ("x", "z"), ("y", "c")
    every = seq + head
    placed = (
        P(seq, head),
        P(seq, None),
        P(seq, None),
        P(),
        P(every, None),
        P(head, None),
        P(),
        P(every, None),
        P(every, None),
        P(every, None, None),
        P(every, None, None),
        P(every, None, None),
    )
    return jax.shard_map(
        local, mesh=mesh, in_specs=placed, out_specs=P(every, None), check_vma=False
    )
```
